128 devices in a mesh: ctx: 16 (over y, x), head: 8 (over z, core).
Axes of the slice: x: 4, y: 4, z: 4, core: 2. Of those that a mesh axis runs over, the one named last changes fastest.
Arguments:
- q_nope: bfloat16 [8, 128, 128], P(None, 'head'), may hold values from -6 to 6
- q_rope: bfloat16 [8, 128, 64], P(None, 'head'), may hold values from -10 to 10
- latent_cache: bfloat16 [8, 131072, 576], P(None, 'ctx'), may hold values from -8 to 8
- lengths: int32 [8], replicated, may hold values from 16384 to 131072, as said below
- w_key_absorb: bfloat16 [128, 128, 512], P('head'), may hold values from -0.5 to 0.5
- w_value_up: bfloat16 [128, 512, 128], P('head'), may hold values from -0.25 to 0.25
- w_output: bfloat16 [16384, 7168], P('head', 'ctx'), may hold values from -0.046875 to 0.046875
- w_gate: bfloat16 [16, 7168, 2048], P('ctx', None, 'head'), may hold values from -0.0625 to 0.0625
- w_up: bfloat16 [16, 7168, 2048], P('ctx', None, 'head'), may hold values from -0.0625 to 0.0625
- w_down: bfloat16 [16, 2048, 7168], P('ctx', 'head'), may hold values from -0.125 to 0.125
- expert_ids: int32 [8, 8], replicated, may hold values from 0 to 15, all different within a row
- gate_weights: float32 [8, 8], replicated, may hold values from 0.05 to 0.4
Outputs:
- attn_out: bfloat16 [8, 7168], P(None, 'ctx')
- expert_out: bfloat16 [8, 7168], P(None, ('ctx', 'head'))
The draws below stay inside these ranges and needn't reach their ends.
Inputs may be any that keep to these rules, and one draw needn't show every extreme that they name: `lengths`: every row has at least 16384 valid positions and row 0 has all of them.
All inputs are finite; a program needn't handle non-finite values.
Results may differ from the reference program's by a relative error of at most 0.03.
Values may be sent and summed in bfloat16 or wider, within the bound.
A program may use at most 192 MiB of HBM per device.

```python
import jax
import jax.numpy as jnp
from jax import lax

D = 7168
HEADS = 128
NOPE = 128
ROPE = 64
LAT = 512
FF = 2048
TOPK = 8
ROWS = 8
LENGTH = 131072
EXP_LIVE = 16


def plan_rows(key, low, high):
    keys = jax.random.split(key, 4)
    signs = jnp.where(jax.random.bernoulli(keys[0], 0.5, (ROWS, ROPE)), 1.0, -1.0).astype(jnp.float32)
    chosen = jax.random.bernoulli(keys[1], 0.25, (ROWS, HEADS)).at[0, 0].set(True).at[1, 0].set(True)
    gains = low + jax.random.uniform(keys[2], (ROWS, HEADS), jnp.float32)
    gains = gains.at[0, 0].set(high)
    spots = jax.random.randint(keys[3], (ROWS,), 0, LENGTH // 16, dtype=jnp.int32)
    spots = spots + jnp.where(jnp.arange(ROWS, dtype=jnp.int32) == 0, LENGTH // 2, 0).astype(jnp.int32)
    return (signs, chosen, gains, spots)


def draw_q_nope(key, part):
    low, high = (0.5, 1.5)
    signs, chosen, gains, spots = plan_rows(key, low, high)
    key = jax.random.fold_in(key, 13)
    base = jnp.clip(jax.random.normal(key, (ROWS, HEADS, NOPE), jnp.float32), -6.0, 6.0)
    return jnp.where(chosen[:, :, None], base, base).astype(jnp.bfloat16)


def draw_q_rope(key, part):
    low, high = (0.5, 1.5)
    signs, chosen, gains, spots = plan_rows(key, low, high)
    key = jax.random.fold_in(key, 17)
    base = jnp.clip(jax.random.normal(key, (ROWS, HEADS, ROPE), jnp.float32), -6.0, 6.0)
    lifted = gains[:, :, None] * signs[:, None, :]
    return jnp.where(chosen[:, :, None], lifted, base).astype(jnp.bfloat16)


def draw_latent_cache(key, part):
    low, high = (0.5, 1.5)
    signs, chosen, gains, spots = plan_rows(key, low, high)
    key = jax.random.fold_in(key, 19)
    base = jnp.clip(jax.random.normal(key, (ROWS, LENGTH, LAT + ROPE), jnp.float32), -6.0, 6.0)
    lifted = jnp.concatenate([jnp.zeros((ROWS, LAT), jnp.float32), signs], axis=1)
    column = jnp.arange(LAT + ROPE, dtype=jnp.int32)[None, None, :] >= LAT
    place = jnp.arange(LENGTH, dtype=jnp.int32)[None, :, None]
    marked = (jnp.arange(ROWS, dtype=jnp.int32) != 1)[:, None, None]
    near = (place == spots[:, None, None]) & column & marked
    far = (place == spots[:, None, None] + LENGTH // 16) & column & marked
    base = jnp.where(near, 8.0 * lifted[:, None, :], base)
    base = jnp.where(far, 7.9375 * lifted[:, None, :], base)
    return base.astype(jnp.bfloat16)


def draw_lengths(key, part):
    key = jax.random.fold_in(key, 5)
    values = jax.random.randint(key, (ROWS,), LENGTH // 8, LENGTH + 1, dtype=jnp.int32)
    return values.at[0].set(LENGTH)


def level_of(own_key, dims, cuts, low, top_value):
    loudness = 1.0
    for dim, parts in cuts:
        steps = jax.random.uniform(jax.random.fold_in(jax.random.fold_in(own_key, 6), dim), (parts,), jnp.float32, low / len(cuts), top_value / len(cuts))
        loudness = loudness * jnp.repeat(jnp.exp(steps), dims[dim] // parts).reshape((-1,) + (1,) * (len(dims) - 1 - dim))
    return loudness


def different_ones(rng, rows, amount, top, lift):
    ranking = jax.random.permutation(jax.random.fold_in(rng, 1), amount)
    pull = ranking
    for power in range(3):
        pull = pull * pull // amount
    pull = pull * lift // amount
    tickets = jax.random.randint(jax.random.fold_in(rng, 2), (rows, amount), 0, 4096) + pull
    holders = jax.random.permutation(jax.random.fold_in(rng, 3), rows)[jnp.arange(amount) % rows]
    tickets = jnp.where(jnp.arange(rows)[:, None] == holders[None, :], 1 << 14, tickets)
    priority = tickets * amount + jnp.arange(amount)
    return lax.top_k(priority.astype(jnp.int32), top)[1].astype(jnp.int32)


def bell_draw(key, dims, width, limit, cuts=(), held_as=jnp.bfloat16):
    drawn = width * jax.random.normal(key, dims, jnp.float32)
    if cuts:
        drawn = drawn * level_of(key, dims, cuts, -0.22, 0.18)
    return jnp.clip(drawn, -limit, limit).astype(held_as)


def setup_inputs(seed: int = 0) -> dict:
    key_list = jax.random.split(jax.random.key(seed), 13)
    q_nope = draw_q_nope(jax.random.fold_in(key_list[12], 71), 0)
    q_rope = draw_q_rope(jax.random.fold_in(key_list[12], 71), 0)
    latent_cache = draw_latent_cache(jax.random.fold_in(key_list[12], 71), 0)
    lengths = draw_lengths(jax.random.fold_in(key_list[12], 71), 0)
    w_key_absorb = bell_draw(key_list[4], (HEADS, NOPE, LAT), NOPE ** -0.5, 0.5, ((0, 8),))
    w_value_up = bell_draw(key_list[5], (HEADS, LAT, NOPE), LAT ** -0.5, 0.25, ((0, 8),))
    w_output = bell_draw(key_list[6], (HEADS * NOPE, D), (HEADS * NOPE) ** -0.5, 0.046875, ((0, 8), (1, 16)))
    w_gate = bell_draw(key_list[7], (EXP_LIVE, D, FF), D ** -0.5, 0.0625, ((0, 16), (2, 8)))
    w_up = bell_draw(key_list[8], (EXP_LIVE, D, FF), D ** -0.5, 0.0625, ((0, 16), (2, 8)))
    w_down = bell_draw(key_list[9], (EXP_LIVE, FF, D), FF ** -0.5, 0.125, ((0, 16), (1, 8)))
    expert_ids = different_ones(key_list[10], ROWS, EXP_LIVE, TOPK, 4096)
    gate_weights = jnp.clip(jax.random.uniform(key_list[11], (ROWS, TOPK), jnp.float32, 0.05, 0.4), 0.05, 0.4)
    return dict(q_nope=q_nope, q_rope=q_rope, latent_cache=latent_cache, lengths=lengths, w_key_absorb=w_key_absorb, w_value_up=w_value_up, w_output=w_output, w_gate=w_gate, w_up=w_up, w_down=w_down, expert_ids=expert_ids, gate_weights=gate_weights)


def reference(q_nope, q_rope, latent_cache, lengths, w_key_absorb, w_value_up, w_output, w_gate, w_up, w_down, expert_ids, gate_weights):
    scale = (NOPE + ROPE) ** (-0.5)
    q_latent = jnp.einsum('bhn,hnl->bhl', q_nope.astype(jnp.float32), w_key_absorb.astype(jnp.float32)).astype(jnp.bfloat16)
    query = jnp.concatenate([q_latent, q_rope], axis=-1)
    positions = jnp.arange(LENGTH, dtype=jnp.int32)

    def one_row(packed):
        query_row, cache_row, length = packed
        score = jnp.dot(query_row, cache_row.T, preferred_element_type=jnp.float32) * scale
        valid = positions[None, :] < length
        top = lax.optimization_barrier(jnp.max(jnp.where(valid, score, -1e+30), axis=-1))
        weight = jnp.where(valid, jnp.exp(score - top[:, None]), 0.0)
        total = lax.optimization_barrier(jnp.sum(weight, axis=-1))
        summed = jnp.dot(weight.astype(jnp.bfloat16), cache_row[:, :LAT], preferred_element_type=jnp.float32)
        return (summed / total[:, None]).astype(jnp.bfloat16)
    o_latent = lax.map(one_row, (query, latent_cache, lengths.astype(jnp.int32)))
    head_out = jnp.einsum('bhl,hln->bhn', o_latent.astype(jnp.float32), w_value_up.astype(jnp.float32)).astype(jnp.bfloat16)
    head_out = head_out.reshape(ROWS, HEADS * NOPE)
    attn_out = jnp.dot(head_out, w_output, preferred_element_type=jnp.float32).astype(jnp.bfloat16)
    wide = attn_out.astype(jnp.float32)
    normed = (wide / jnp.sqrt(lax.optimization_barrier(jnp.mean(wide * wide, axis=-1, keepdims=True)) + 1e-06)).astype(jnp.bfloat16)
    experts = jnp.arange(EXP_LIVE, dtype=jnp.int32)
    select = lax.optimization_barrier(jnp.sum(gate_weights[:, :, None] * (expert_ids[:, :, None] == experts[None, None, :]).astype(jnp.float32), axis=1))

    def one_expert(carry, packed):
        gate_w, up_w, down_w, weighting = packed
        gate = jnp.dot(normed, gate_w, preferred_element_type=jnp.float32)
        upper = jnp.dot(normed, up_w, preferred_element_type=jnp.float32)
        hidden = (jax.nn.silu(gate) * upper).astype(jnp.bfloat16)
        result = jnp.dot(hidden, down_w, preferred_element_type=jnp.float32)
        return (carry + weighting[:, None] * result, None)
    summed, _ = lax.scan(one_expert, jnp.zeros((ROWS, D), jnp.float32), (w_gate, w_up, w_down, select.T))
    return (attn_out, summed.astype(jnp.bfloat16))
```

```python
import functools
import math

import jax
import jax.numpy as jnp
from jax import lax
from jax.experimental import pallas as pl
from jax.experimental.pallas import tpu as pltpu
from jax.sharding import PartitionSpec as P

ROWS = 8
HEADS = 128
NOPE = 128
ROPE = 64
LAT = 512
KEY = LAT + ROPE
D = 7168
CTX = 16
HEAD = 8
GROUP = HEADS // HEAD
SPAN = 8192 // HEAD
COLS = D // CTX
OUT = COLS // HEAD
CHUNK = 2
CHUNKS = ROWS // CHUNK
TILES = CHUNK * 4 + 1
SCALE = (NOPE + ROPE) ** -0.5 * math.log2(math.e)
MESH = pl.DeviceIdType.MESH
F32 = jnp.float32
BF16 = jnp.bfloat16


def remote(src, dst, send_sem, recv_sem, device):
    return pltpu.make_async_remote_copy(
        src_ref=src,
        dst_ref=dst,
        send_sem=send_sem,
        recv_sem=recv_sem,
        device_id=device,
        device_id_type=MESH,
    )


def loop(low, high, step):
    def run(index, carry):
        step(index)
        return carry

    lax.fori_loop(low, high, run, 0)


def pack(wide):
    wide = wide.astype(BF16).astype(F32)
    first = jnp.concatenate([wide[:, 0:128], wide[:, 128:256]], axis=0).astype(BF16)
    second = jnp.concatenate([wide[:, 256:384], wide[:, 384:512]], axis=0).astype(BF16)
    return first, second


def unpack(first, second):
    first = first.astype(F32)
    second = second.astype(F32)
    return jnp.concatenate([first[0:8], first[8:16], second[0:8], second[8:16]], axis=1)


def split_three(value):
    high = value.astype(BF16).astype(F32)
    rest = value - high
    middle = rest.astype(BF16).astype(F32)
    return high, middle, rest - middle


def lanes(shape):
    return lax.broadcasted_iota(jnp.int32, shape, len(shape) - 1)


def put_levels(levels, rows):
    lane = lanes((rows, 128))
    tile = jnp.zeros((rows, 128), F32)
    for index, level in enumerate(levels):
        for part, value in enumerate(split_three(level)):
            tile = jnp.where(lane == 3 * index + part, value, tile)
    return tile


def get_level(tile, index):
    lane = lanes(tile.shape)
    wanted = (lane >= 3 * index) & (lane < 3 * index + 3)
    return jnp.sum(jnp.where(wanted, tile, 0.0), axis=1, keepdims=True)


def weights_of(levels):
    peak = functools.reduce(jnp.maximum, levels)
    parts = [jnp.exp2(level - peak) for level in levels]
    total = functools.reduce(jnp.add, parts)
    scale = 1.0 / total
    return [part * scale for part in parts], peak + jnp.log2(total)


def kernel(
    lengths_ref,
    q_nope_ref,
    q_rope_ref,
    ids_ref,
    gates_ref,
    cache_hbm,
    absorb_hbm,
    value_hbm,
    output_hbm,
    gate_hbm,
    up_hbm,
    down_hbm,
    attn_ref,
    expert_ref,
    keys,
    absorb,
    value_up,
    w_out,
    w_gate,
    w_up,
    w_down,
    query,
    s1,
    r1,
    s2,
    r2,
    whole,
    whole_level,
    s3,
    r3,
    s4,
    r4,
    s5,
    r5,
    s6,
    r6,
    s7,
    r7,
    s8,
    r8,
    key_sem,
    weight_sem,
    q_send,
    q_from_z,
    q_from_mate,
    s1_sem,
    r1_sem,
    s2_sem,
    r2_sem,
    s3_sem,
    r3_sem,
    s4_sem,
    r4_sem,
    s5_sem,
    r5_sem,
    s6_sem,
    r6_sem,
    s7_sem,
    r7_sem,
    s8_sem,
    r8_sem,
):
    ctx = lax.axis_index("ctx")
    head = lax.axis_index("head")
    level_z = head // 2
    core = lax.rem(head, 2)
    mate = level_z * 2 + 1 - core

    def other_z(step):
        return lax.rem(level_z + step, 4)

    def other_ctx(step):
        return lax.rem(ctx + step, CTX)

    def other_head(step):
        return lax.rem(head + step, HEAD)

    absorb_copy = pltpu.make_async_copy(absorb_hbm, absorb, weight_sem.at[0])
    absorb_copy.start()
    start = pl.multiple_of(head * SPAN, SPAN)

    def key_copy(row):
        return pltpu.make_async_copy(
            cache_hbm.at[row, :, pl.ds(start, SPAN)], keys.at[row], key_sem.at[row]
        )

    loop(0, ROWS, lambda row: key_copy(row).start())
    value_copy = pltpu.make_async_copy(value_hbm.at[ctx], value_up, weight_sem.at[1])
    output_copy = pltpu.make_async_copy(output_hbm, w_out.at[pl.ds(0, COLS)], weight_sem.at[2])
    gate_copy = pltpu.make_async_copy(gate_hbm.at[0], w_gate, weight_sem.at[3])
    up_copy = pltpu.make_async_copy(up_hbm.at[0], w_up, weight_sem.at[4])
    down_copy = pltpu.make_async_copy(down_hbm.at[0], w_down, weight_sem.at[5])
    for copy in (value_copy, output_copy, gate_copy, up_copy, down_copy):
        copy.start()

    barrier = pltpu.get_barrier_semaphore()

    def greet_head(step):
        pl.semaphore_signal(
            barrier, inc=1, device_id={"head": other_head(step)}, device_id_type=MESH
        )

    def greet_ctx(step):
        pl.semaphore_signal(
            barrier, inc=1, device_id={"ctx": other_ctx(step)}, device_id_type=MESH
        )

    loop(1, HEAD, greet_head)
    loop(1, CTX, greet_ctx)

    w_out[pl.ds(COLS, 512 - COLS), :] = jnp.zeros((512 - COLS, GROUP * NOPE), BF16)
    flat = q_nope_ref[...].reshape(ROWS * GROUP, NOPE).astype(F32)
    which = lax.rem(lax.broadcasted_iota(jnp.int32, (ROWS * GROUP, NOPE), 0), GROUP)
    blocks = [jnp.where(which == h, flat, 0.0).astype(BF16) for h in range(GROUP)]
    wide_query = jnp.concatenate(blocks, axis=1)
    absorb_copy.wait()
    latent = jnp.dot(
        wide_query,
        absorb[...].reshape(GROUP * NOPE, LAT),
        preferred_element_type=F32,
    ).astype(BF16)
    mine = pl.ds(pl.multiple_of(head * GROUP, GROUP), GROUP)
    query[:, mine, 0:LAT] = latent.reshape(ROWS, GROUP, LAT)
    query[:, mine, LAT:KEY] = q_rope_ref[...]
    pl.semaphore_wait(barrier, HEAD - 1 + CTX - 1)

    def query_block(chunk, source):
        rows = pl.ds(chunk * CHUNK, CHUNK)
        return query.at[rows, pl.ds(pl.multiple_of(source * GROUP, GROUP), GROUP)]

    def query_to_z(chunk, step):
        block = query_block(chunk, head)
        z = other_z(step)
        return remote(
            block, block, q_send.at[chunk, step], q_from_z.at[chunk, level_z], {"head": z * 2 + core}
        )

    def query_from_z(chunk, step):
        z = other_z(step)
        block = query_block(chunk, z * 2 + core)
        return remote(
            block, block, q_send.at[chunk, step], q_from_z.at[chunk, z], {"head": z * 2 + core}
        )

    def query_to_mate(chunk, step):
        z = other_z(step)
        block = query_block(chunk, z * 2 + core)
        return remote(
            block, block, q_send.at[chunk, 4 + step], q_from_mate.at[chunk, z], {"head": mate}
        )

    def query_from_mate(chunk, step):
        z = other_z(step)
        block = query_block(chunk, z * 2 + 1 - core)
        return remote(
            block, block, q_send.at[chunk, 4 + step], q_from_mate.at[chunk, z], {"head": mate}
        )

    def send_query(chunk):
        query_to_mate(chunk, 0).start()
        loop(1, 4, lambda step: query_to_z(chunk, step).start())

    loop(0, CHUNKS, send_query)

    def forward_query(chunk):
        def one(step):
            query_from_z(chunk, step).wait_recv()
            query_to_mate(chunk, step).start()

        loop(1, 4, one)

    def receive_query(chunk):
        loop(0, 4, lambda step: query_from_mate(chunk, step).wait_recv())

    base = ctx * (SPAN * HEAD) + head * SPAN
    position = base + lanes((1, SPAN))

    def attend_row(row):
        key_copy(row).wait()
        block = keys[row]
        score = jnp.dot(query[row], block, preferred_element_type=F32)
        score = jnp.where(position < lengths_ref[row], score, -1e30)
        peak = jnp.max(score, axis=1, keepdims=True)
        weight = jnp.exp2((score - peak) * SCALE)
        total = jnp.sum(weight, axis=1, keepdims=True)
        summed = lax.dot_general(
            weight.astype(BF16),
            block[:LAT],
            (((1,), (1,)), ((), ())),
            preferred_element_type=F32,
        )
        return summed * (1.0 / total), peak * SCALE + jnp.log2(total)

    def first_copy(chunk):
        return remote(
            s1.at[chunk, 1 - core], r1.at[chunk], s1_sem.at[chunk], r1_sem.at[chunk], {"head": mate}
        )

    def attend(chunk):
        results = [attend_row(chunk * CHUNK + row) for row in range(CHUNK)]
        level = put_levels([result[1] for result in results], HEADS)
        for group in range(HEAD):
            rows = slice(group * GROUP, (group + 1) * GROUP)
            for row in range(CHUNK):
                for tile in range(4):
                    s1[chunk, group % 2, group // 2, row * 4 + tile] = results[row][0][
                        rows, tile * 128 : (tile + 1) * 128
                    ].astype(BF16)
            s1[chunk, group % 2, group // 2, CHUNK * 4] = level[rows].astype(BF16)
        first_copy(chunk).start()

    def merge(blocks):
        tiles = [block[CHUNK * 4].astype(F32) for block in blocks]
        merged, levels = [], []
        for row in range(CHUNK):
            parts, level = weights_of([get_level(tile, row) for tile in tiles])
            levels.append(level)
            merged.append(
                [
                    functools.reduce(
                        jnp.add,
                        [
                            block[row * 4 + tile].astype(F32) * part
                            for block, part in zip(blocks, parts)
                        ],
                    )
                    for tile in range(4)
                ]
            )
        return merged, levels

    def second_copy(chunk, step):
        z = other_z(step)
        return remote(
            s2.at[chunk, z],
            r2.at[chunk, level_z],
            s2_sem.at[chunk, step],
            r2_sem.at[chunk, level_z],
            {"head": z * 2 + core},
        )

    def second_arrival(chunk, step):
        z = other_z(step)
        return remote(
            s2.at[chunk, z],
            r2.at[chunk, z],
            s2_sem.at[chunk, step],
            r2_sem.at[chunk, z],
            {"head": z * 2 + core},
        )

    def merge_cores(chunk):
        first_copy(chunk).wait_recv()

        def one(step):
            z = other_z(step)
            merged, levels = merge([s1.at[chunk, core, z], r1.at[chunk, z]])
            for row in range(CHUNK):
                for tile in range(4):
                    s2[chunk, z, row * 4 + tile] = merged[row][tile].astype(BF16)
            s2[chunk, z, CHUNK * 4] = put_levels(levels, GROUP).astype(BF16)

        def send(step):
            one(step)
            second_copy(chunk, step).start()

        loop(1, 4, send)
        one(0)

    def merge_z(chunk):
        loop(1, 4, lambda step: second_arrival(chunk, step).wait_recv())
        sources = [s2.at[chunk, level_z]] + [r2.at[chunk, other_z(step)] for step in (1, 2, 3)]
        merged, levels = merge(sources)
        for row in range(CHUNK):
            rows = pl.ds(pl.multiple_of((chunk * CHUNK + row) * GROUP, GROUP), GROUP)
            for tile in range(4):
                whole[tile, rows, :] = merged[row][tile]
            whole_level[rows, :] = jnp.broadcast_to(levels[row], (GROUP, 128))

    def stage(index):
        @pl.when(index < CHUNKS)
        def _():
            forward_query(index)

        @pl.when((index >= 1) & (index <= CHUNKS))
        def _():
            receive_query(index - 1)
            attend(index - 1)

        @pl.when((index >= 2) & (index <= CHUNKS + 1))
        def _():
            merge_cores(index - 2)

        @pl.when(index >= 3)
        def _():
            merge_z(index - 3)

    loop(0, CHUNKS + 3, stage)

    def to_ctx(src, dst, send_sem, recv_sem, step):
        peer = other_ctx(step)
        return remote(src(peer), dst.at[ctx], send_sem.at[peer], recv_sem.at[ctx], {"ctx": peer})

    def from_ctx(src, dst, send_sem, recv_sem, step):
        peer = other_ctx(step)
        return remote(src(peer), dst.at[peer], send_sem.at[peer], recv_sem.at[peer], {"ctx": peer})

    def to_head(src, dst, send_sem, recv_sem, step):
        peer = other_head(step)
        return remote(src(peer), dst.at[head], send_sem.at[peer], recv_sem.at[head], {"head": peer})

    def from_head(src, dst, send_sem, recv_sem, step):
        peer = other_head(step)
        return remote(src(peer), dst.at[peer], send_sem.at[peer], recv_sem.at[peer], {"head": peer})

    for member in range(GROUP):
        rows = pl.ds(member, ROWS, stride=GROUP)
        first, second = pack(jnp.concatenate([whole[tile, rows, :] for tile in range(4)], axis=1))
        s3[member, 0] = first
        s3[member, 1] = second
        level = put_levels([whole_level[rows, :]], ROWS)
        s3[member, 2] = jnp.concatenate([level, jnp.zeros_like(level)], axis=0).astype(BF16)
    exchange3 = (lambda peer: s3.at[peer], r3, s3_sem, r3_sem)
    loop(1, CTX, lambda step: to_ctx(*exchange3, step).start())
    r3[ctx] = s3[ctx]
    value_copy.wait()
    loop(1, CTX, lambda step: from_ctx(*exchange3, step).wait_recv())
    parts, _ = weights_of([get_level(r3[peer, 2].astype(F32)[0:8], 0) for peer in range(CTX)])
    latent_out = functools.reduce(
        jnp.add, [unpack(r3[peer, 0], r3[peer, 1]) * parts[peer] for peer in range(CTX)]
    )
    head_out = jnp.dot(latent_out.astype(BF16), value_up[...], preferred_element_type=F32)
    s4[...] = head_out.astype(BF16).astype(F32)
    exchange4 = (lambda peer: s4, r4, s4_sem, r4_sem)
    loop(1, CTX, lambda step: to_ctx(*exchange4, step).start())
    r4[ctx] = s4[...]
    output_copy.wait()
    loop(1, CTX, lambda step: from_ctx(*exchange4, step).wait_recv())
    gathered = jnp.concatenate([r4[peer] for peer in range(CTX)], axis=1).astype(BF16)
    partial = lax.dot_general(
        gathered, w_out[...], (((1,), (1,)), ((), ())), preferred_element_type=F32
    )
    first, second = pack(partial)
    s5[0] = first
    s5[1] = second
    exchange5 = (lambda peer: s5, r5, s5_sem, r5_sem)
    loop(1, HEAD, lambda step: to_head(*exchange5, step).start())
    r5[head] = s5[...]
    loop(1, HEAD, lambda step: from_head(*exchange5, step).wait_recv())
    attn = functools.reduce(jnp.add, [unpack(r5[peer, 0], r5[peer, 1]) for peer in range(HEAD)])
    first, second = pack(attn)
    s6[0] = first
    s6[1] = second
    exchange6 = (lambda peer: s6, r6, s6_sem, r6_sem)
    loop(1, CTX, lambda step: to_ctx(*exchange6, step).start())
    r6[ctx] = s6[...]
    attn_ref[...] = attn[:, 0:COLS].astype(BF16)
    gate_copy.wait()
    up_copy.wait()
    loop(1, CTX, lambda step: from_ctx(*exchange6, step).wait_recv())
    squares = jnp.zeros((ROWS, 512), F32)
    gate = jnp.zeros((ROWS, 256), F32)
    upper = jnp.zeros((ROWS, 256), F32)
    for peer in range(CTX):
        features = unpack(r6[peer, 0], r6[peer, 1])
        squares += features * features
        features = features[:, 0:COLS].astype(BF16)
        rows = pl.ds(peer * COLS, COLS)
        gate += jnp.dot(features, w_gate[rows, :], preferred_element_type=F32)
        upper += jnp.dot(features, w_up[rows, :], preferred_element_type=F32)
    mean = jnp.sum(squares, axis=1, keepdims=True) * (1.0 / D)
    factor = 1.0 / jnp.sqrt(mean + 1e-06)
    gate = gate * factor
    upper = upper * factor
    hidden = (gate / (1.0 + jnp.exp(-gate)) * upper).astype(BF16)
    chosen = jnp.where(ids_ref[...] == ctx, gates_ref[...], 0.0)
    select = jnp.sum(chosen, axis=1, keepdims=True)
    down_copy.wait()
    result = jnp.dot(hidden, w_down[...], preferred_element_type=F32) * select
    for peer in range(CTX):
        left = peer * COLS // 128 * 128
        first, second = pack(result[:, left : left + 512])
        s7[peer, 0] = first
        s7[peer, 1] = second
    exchange7 = (lambda peer: s7.at[peer], r7, s7_sem, r7_sem)
    loop(1, CTX, lambda step: to_ctx(*exchange7, step).start())
    r7[ctx] = s7[ctx]
    loop(1, CTX, lambda step: from_ctx(*exchange7, step).wait_recv())
    share = functools.reduce(jnp.add, [unpack(r7[peer, 0], r7[peer, 1]) for peer in range(CTX)])
    share = jnp.where(lax.rem(ctx, 2) == 1, pltpu.roll(share, 512 - COLS % 128, 1), share)
    for peer in range(HEAD):
        moved = share if peer == 0 else pltpu.roll(share, 512 - peer * OUT, 1)
        s8[peer] = moved[:, 0:128]
    exchange8 = (lambda peer: s8.at[peer], r8, s8_sem, r8_sem)
    loop(1, HEAD, lambda step: to_head(*exchange8, step).start())
    r8[head] = s8[head]
    loop(1, HEAD, lambda step: from_head(*exchange8, step).wait_recv())
    final = functools.reduce(jnp.add, [r8[peer] for peer in range(HEAD)])
    expert_ref[...] = final[:, 0:OUT].astype(BF16)

    def drain(chunk):
        def queries(step):
            query_to_z(chunk, step).wait_send()
            query_to_mate(chunk, step).wait_send()
            second_copy(chunk, step).wait_send()

        loop(1, 4, queries)
        query_to_mate(chunk, 0).wait_send()
        first_copy(chunk).wait_send()

    loop(0, CHUNKS, drain)

    def drain_ctx(step):
        for exchange in (exchange3, exchange4, exchange6, exchange7):
            to_ctx(*exchange, step).wait_send()

    def drain_head(step):
        for exchange in (exchange5, exchange8):
            to_head(*exchange, step).wait_send()

    loop(1, CTX, drain_ctx)
    loop(1, HEAD, drain_head)


def body(
    q_nope,
    q_rope,
    latent_cache,
    lengths,
    w_key_absorb,
    w_value_up,
    w_output,
    w_gate,
    w_up,
    w_down,
    expert_ids,
    gate_weights,
):
    vmem = pl.BlockSpec(memory_space=pltpu.VMEM)
    hbm = pl.BlockSpec(memory_space=pl.ANY)
    dma = pltpu.SemaphoreType.DMA
    return pl.pallas_call(
        kernel,
        out_shape=(
            jax.ShapeDtypeStruct((ROWS, COLS), BF16),
            jax.ShapeDtypeStruct((ROWS, OUT), BF16),
        ),
        in_specs=[pl.BlockSpec(memory_space=pltpu.SMEM)] + [vmem] * 4 + [hbm] * 7,
        out_specs=(vmem, vmem),
        scratch_shapes=[
            pltpu.VMEM((ROWS, KEY, SPAN), BF16),
            pltpu.VMEM((GROUP, NOPE, LAT), BF16),
            pltpu.VMEM((LAT, NOPE), BF16),
            pltpu.VMEM((512, GROUP * NOPE), BF16),
            pltpu.VMEM((D, 256), BF16),
            pltpu.VMEM((D, 256), BF16),
            pltpu.VMEM((256, D), BF16),
            pltpu.VMEM((ROWS, HEADS, KEY), BF16),
            pltpu.VMEM((CHUNKS, 2, 4, TILES, 16, 128), BF16),
            pltpu.VMEM((CHUNKS, 4, TILES, 16, 128), BF16),
            pltpu.VMEM((CHUNKS, 4, TILES, 16, 128), BF16),
            pltpu.VMEM((CHUNKS, 4, TILES, 16, 128), BF16),
            pltpu.VMEM((4, ROWS * GROUP, 128), F32),
            pltpu.VMEM((ROWS * GROUP, 128), F32),
            pltpu.VMEM((CTX, 3, 16, 128), BF16),
            pltpu.VMEM((CTX, 3, 16, 128), BF16),
            pltpu.VMEM((ROWS, NOPE), F32),
            pltpu.VMEM((CTX, ROWS, NOPE), F32),
            pltpu.VMEM((2, 16, 128), BF16),
            pltpu.VMEM((HEAD, 2, 16, 128), BF16),
            pltpu.VMEM((2, 16, 128), BF16),
            pltpu.VMEM((CTX, 2, 16, 128), BF16),
            pltpu.VMEM((CTX, 2, 16, 128), BF16),
            pltpu.VMEM((CTX, 2, 16, 128), BF16),
            pltpu.VMEM((HEAD, ROWS, 128), F32),
            pltpu.VMEM((HEAD, ROWS, 128), F32),
            dma((ROWS,)),
            dma((6,)),
            dma((CHUNKS, 8)),
            dma((CHUNKS, 4)),
            dma((CHUNKS, 4)),
            dma((CHUNKS,)),
            dma((CHUNKS,)),
            dma((CHUNKS, 4)),
            dma((CHUNKS, 4)),
            dma((CTX,)),
            dma((CTX,)),
            dma((CTX,)),
            dma((CTX,)),
            dma((HEAD,)),
            dma((HEAD,)),
            dma((CTX,)),
            dma((CTX,)),
            dma((CTX,)),
            dma((CTX,)),
            dma((HEAD,)),
            dma((HEAD,)),
        ],
        compiler_params=pltpu.CompilerParams(
            collective_id=0, has_side_effects=True, vmem_limit_bytes=56 * 2**20
        ),
    )(
        lengths,
        q_nope,
        q_rope,
        expert_ids,
        gate_weights,
        jnp.swapaxes(latent_cache, 1, 2),
        w_key_absorb,
        w_value_up,
        w_output.T,
        w_gate,
        w_up,
        w_down,
    )


def solution(mesh):
    return jax.shard_map(
        body,
        mesh=mesh,
        in_specs=(
            P(None, "head", None),
            P(None, "head", None),
            P(None, "ctx", None),
            P(),
            P("head", None, None),
            P("head", None, None),
            P("head", "ctx"),
            P("ctx", None, "head"),
            P("ctx", None, "head"),
            P("ctx", "head", None),
            P(),
            P(),
        ),
        out_specs=(P(None, "ctx"), P(None, ("ctx", "head"))),
        check_vma=False,
    )
```

```python
import functools
import math

import jax
import jax.numpy as jnp
from jax import lax
from jax.experimental import pallas as pl
from jax.experimental.pallas import tpu as pltpu
from jax.sharding import PartitionSpec as P

ROWS = 8
HEADS = 128
NOPE = 128
ROPE = 64
LAT = 512
KEY = LAT + ROPE
D = 7168
CTX = 16
HEAD = 8
GROUP = HEADS // HEAD
SPAN = 8192 // 2
SLOTS = 6
COLS = D // CTX
OUT = COLS // HEAD
CHUNK = 2
CHUNKS = ROWS // CHUNK
TRANSPOSED = (((1,), (1,)), ((), ()))
TILES = CHUNK * 4 + 1
SCALE = (NOPE + ROPE) ** -0.5 * math.log2(math.e)
EARLY = 6
LATE = ROWS - EARLY
MESH = pl.DeviceIdType.MESH
F32 = jnp.float32
BF16 = jnp.bfloat16


def remote(src, dst, send_sem, recv_sem, device):
    return pltpu.make_async_remote_copy(
        src_ref=src,
        dst_ref=dst,
        send_sem=send_sem,
        recv_sem=recv_sem,
        device_id=device,
        device_id_type=MESH,
    )


def hops(step):
    return sum(min(part, 4 - part) for part in step)


NEAREST = sorted(((dy, dx) for dy in range(4) for dx in range(4) if dy or dx), key=hops)
FARTHEST = NEAREST[::-1]


def loop(low, high, step):
    def run(index, carry):
        step(index)
        return carry

    lax.fori_loop(low, high, run, 0)


def pack(wide):
    wide = wide.astype(BF16).astype(F32)
    first = jnp.concatenate([wide[:, 0:128], wide[:, 128:256]], axis=0).astype(BF16)
    second = jnp.concatenate([wide[:, 256:384], wide[:, 384:512]], axis=0).astype(BF16)
    return first, second


def unpack(first, second):
    first = first.astype(F32)
    second = second.astype(F32)
    return jnp.concatenate([first[0:8], first[8:16], second[0:8], second[8:16]], axis=1)


def split_three(value):
    high = value.astype(BF16).astype(F32)
    rest = value - high
    middle = rest.astype(BF16).astype(F32)
    return high, middle, rest - middle


def lanes(shape):
    return lax.broadcasted_iota(jnp.int32, shape, len(shape) - 1)


def put_levels(levels, rows):
    lane = lanes((rows, 128))
    tile = jnp.zeros((rows, 128), F32)
    for index, level in enumerate(levels):
        for part, value in enumerate(split_three(level)):
            tile = jnp.where(lane == 3 * index + part, value, tile)
    return tile


def get_level(tile, index):
    lane = lanes(tile.shape)
    wanted = (lane >= 3 * index) & (lane < 3 * index + 3)
    return jnp.sum(jnp.where(wanted, tile, 0.0), axis=1, keepdims=True)


def weights_of(levels):
    peak = functools.reduce(jnp.maximum, levels)
    parts = [jnp.exp2(level - peak) for level in levels]
    total = functools.reduce(jnp.add, parts)
    scale = 1.0 / total
    return [part * scale for part in parts], peak + jnp.log2(total)


def kernel(
    lengths_ref,
    q_nope_ref,
    q_rope_ref,
    ids_ref,
    gates_ref,
    cache_hbm,
    absorb_hbm,
    value_hbm,
    output_hbm,
    gate_hbm,
    up_hbm,
    down_hbm,
    attn_ref,
    expert_ref,
    keys,
    absorb,
    value_up,
    w_out,
    w_gate,
    w_up,
    w_down,
    query,
    s1,
    r1,
    whole,
    whole_level,
    s3,
    r3,
    s4,
    r4,
    heads,
    s5,
    r5,
    s6,
    r6,
    s7,
    r7,
    s8,
    r8,
    key_sem,
    weight_sem,
    query_sem,
    s1_sem,
    r1_sem,
    s3_sem,
    r3_sem,
    s4_sem,
    r4_sem,
    s5_sem,
    r5_sem,
    s6_sem,
    r6_sem,
    s7_sem,
    r7_sem,
    s8_sem,
    r8_sem,
):
    ctx = lax.axis_index("ctx")
    head = lax.axis_index("head")
    core = lax.rem(head, 2)
    mate = {"head": head + 1 - 2 * core}

    def other_ctx(step):
        dy, dx = step
        return lax.rem(ctx // 4 + dy, 4) * 4 + lax.rem(lax.rem(ctx, 4) + dx, 4)

    def other_head(step):
        return lax.rem(head + step, HEAD)

    def key_copy(row):
        return pltpu.make_async_copy(
            cache_hbm.at[row, :, pl.ds(pl.multiple_of(core * SPAN, SPAN), SPAN)],
            keys.at[lax.rem(row, SLOTS)],
            key_sem.at[row],
        )

    absorb_copy = pltpu.make_async_copy(absorb_hbm, absorb, weight_sem.at[0])
    value_copy = pltpu.make_async_copy(value_hbm, value_up, weight_sem.at[1])
    output_copy = pltpu.make_async_copy(output_hbm, w_out.at[pl.ds(0, COLS)], weight_sem.at[2])
    gate_copy = pltpu.make_async_copy(gate_hbm.at[0], w_gate, weight_sem.at[3])
    up_copy = pltpu.make_async_copy(up_hbm.at[0], w_up, weight_sem.at[4])
    down_copy = pltpu.make_async_copy(down_hbm.at[0], w_down, weight_sem.at[5])
    absorb_copy.start()
    barrier = pltpu.get_barrier_semaphore()

    def greet(device):
        pl.semaphore_signal(barrier, inc=1, device_id=device, device_id_type=MESH)

    for step in FARTHEST:
        greet({"ctx": other_ctx(step)})
    loop(1, HEAD, lambda step: greet({"head": other_head(step)}))
    loop(0, SLOTS, lambda row: key_copy(row).start())
    value_copy.start()
    output_copy.start()

    w_out[pl.ds(COLS, 512 - COLS), :] = jnp.zeros((512 - COLS, GROUP * NOPE), BF16)
    flat = q_nope_ref[...].reshape(ROWS * GROUP, NOPE).astype(F32)
    which = lax.rem(lax.broadcasted_iota(jnp.int32, (ROWS * GROUP, NOPE), 0), GROUP)
    blocks = [jnp.where(which == h, flat, 0.0).astype(BF16) for h in range(GROUP)]
    wide_query = jnp.concatenate(blocks, axis=1)
    absorb_copy.wait()
    latent = jnp.dot(
        wide_query,
        absorb[...].reshape(GROUP * NOPE, LAT),
        preferred_element_type=F32,
    ).astype(BF16)
    mine = pl.ds(pl.multiple_of(core * GROUP, GROUP), GROUP)
    query[:, mine, 0:LAT] = latent.reshape(ROWS, GROUP, LAT)
    query[:, mine, LAT:KEY] = q_rope_ref[...]
    pl.semaphore_wait(barrier, HEAD - 1 + CTX - 1)
    query_copy = remote(
        query.at[:, mine], query.at[:, mine], query_sem.at[0], query_sem.at[1], mate
    )
    query_copy.start()
    query_copy.wait_recv()

    position = ctx * (2 * SPAN) + core * SPAN + lanes((1, SPAN))

    def attend_row(row):
        key_copy(row).wait()
        block = keys.at[lax.rem(row, SLOTS)]
        score = jnp.dot(query[row], block[...], preferred_element_type=F32)
        score = jnp.where(position < lengths_ref[row], score, -1e30)
        peak = jnp.max(score, axis=1, keepdims=True)
        weight = jnp.exp2((score - peak) * SCALE)
        total = jnp.sum(weight, axis=1, keepdims=True)
        summed = lax.dot_general(
            block[0:LAT], weight.astype(BF16), TRANSPOSED, preferred_element_type=F32
        )
        return summed.T * (1.0 / total), peak * SCALE + jnp.log2(total)

    def first_copy(chunk):
        return remote(
            s1.at[chunk, 1 - core], r1.at[chunk], s1_sem.at[chunk], r1_sem.at[chunk], mate
        )

    def attend(chunk):
        results = [attend_row(chunk * CHUNK + row) for row in range(CHUNK)]
        level = put_levels([result[1] for result in results], 2 * GROUP)
        for group in range(2):
            rows = slice(group * GROUP, (group + 1) * GROUP)
            for row in range(CHUNK):
                for tile in range(4):
                    s1[chunk, group, row * 4 + tile] = results[row][0][
                        rows, tile * 128 : (tile + 1) * 128
                    ].astype(BF16)
            s1[chunk, group, CHUNK * 4] = level[rows].astype(BF16)
        first_copy(chunk).start()

    def merge_cores(chunk):
        first_copy(chunk).wait_recv()
        blocks = [s1.at[chunk, core], r1.at[chunk]]
        tiles = [block[CHUNK * 4].astype(F32) for block in blocks]
        for row in range(CHUNK):
            parts, level = weights_of([get_level(tile, row) for tile in tiles])
            rows = pl.ds(pl.multiple_of((chunk * CHUNK + row) * GROUP, GROUP), GROUP)
            for tile in range(4):
                whole[rows, tile * 128 : (tile + 1) * 128] = functools.reduce(
                    jnp.add,
                    [
                        block[row * 4 + tile].astype(F32) * part
                        for block, part in zip(blocks, parts)
                    ],
                )
            whole_level[rows, :] = jnp.broadcast_to(level, (GROUP, 128))

    def to_ctx(src, dst, send_sem, recv_sem, step):
        peer = other_ctx(step)
        return remote(src(peer), dst.at[ctx], send_sem.at[peer], recv_sem.at[ctx], {"ctx": peer})

    def from_ctx(src, dst, send_sem, recv_sem, step):
        peer = other_ctx(step)
        return remote(src(peer), dst.at[peer], send_sem.at[peer], recv_sem.at[peer], {"ctx": peer})

    def to_head(src, dst, send_sem, recv_sem, step):
        peer = other_head(step)
        return remote(src(peer), dst.at[head], send_sem.at[peer], recv_sem.at[head], {"head": peer})

    def from_head(src, dst, send_sem, recv_sem, step):
        peer = other_head(step)
        return remote(src(peer), dst.at[peer], send_sem.at[peer], recv_sem.at[peer], {"head": peer})

    exchange3 = (lambda peer: s3, r3, s3_sem, r3_sem)
    exchange4 = (lambda peer: s4, r4, s4_sem, r4_sem)
    exchange5 = (lambda peer: s5, r5, s5_sem, r5_sem)
    exchange6 = (lambda peer: s6, r6, s6_sem, r6_sem)
    exchange7 = (lambda peer: s7.at[peer], r7, s7_sem, r7_sem)
    exchange8 = (lambda peer: s8.at[peer], r8, s8_sem, r8_sem)

    def send_ctx(exchange):
        for step in FARTHEST:
            to_ctx(*exchange, step).start()

    def receive_ctx(exchange):
        for step in NEAREST:
            from_ctx(*exchange, step).wait_recv()

    def project(first, count, exchange):
        rows = pl.ds(first * GROUP, count * GROUP)
        merged = whole[rows, :]
        which = lax.rem(lax.broadcasted_iota(jnp.int32, (count * GROUP, LAT), 0), GROUP)
        blocks = [jnp.where(which == h, merged, 0.0).astype(BF16) for h in range(GROUP)]
        share = jnp.dot(
            jnp.concatenate(blocks, axis=1),
            value_up[...].reshape(GROUP * LAT, NOPE),
            preferred_element_type=F32,
        ).astype(BF16)
        src = exchange[0](0)
        src[0:count] = share.reshape(count, GROUP, NOPE)
        levels = [whole_level[pl.ds((first + row) * GROUP, GROUP), :] for row in range(count)]
        src[count] = put_levels(levels, GROUP).astype(BF16)
        send_ctx(exchange)
        exchange[1][ctx] = src[...]

    def merge_ctx(first, count, exchange):
        receive_ctx(exchange)
        arrived = exchange[1]
        tiles = [arrived[peer, count].astype(F32) for peer in range(CTX)]
        for row in range(count):
            parts, _ = weights_of([get_level(tile, row) for tile in tiles])
            heads[pl.ds((first + row) * GROUP, GROUP), :] = functools.reduce(
                jnp.add, [arrived[peer, row].astype(F32) * parts[peer] for peer in range(CTX)]
            )

    def stage(chunk):
        attend(chunk)

        @pl.when(chunk == 0)
        def _():
            loop(SLOTS, ROWS, lambda row: key_copy(row).start())
            gate_copy.start()
            up_copy.start()
            down_copy.start()

        @pl.when(chunk >= 1)
        def _():
            merge_cores(chunk - 1)

    loop(0, CHUNKS - 1, stage)
    merge_cores(CHUNKS - 2)
    value_copy.wait()
    project(0, EARLY, exchange3)
    attend(CHUNKS - 1)
    merge_cores(CHUNKS - 1)
    project(EARLY, LATE, exchange4)
    merge_ctx(0, EARLY, exchange3)
    output_copy.wait()
    merge_ctx(EARLY, LATE, exchange4)
    gathered = [heads[pl.ds(member, ROWS, stride=GROUP), :] for member in range(GROUP)]
    partial = lax.dot_general(
        jnp.concatenate(gathered, axis=1).astype(BF16),
        w_out[...],
        TRANSPOSED,
        preferred_element_type=F32,
    )
    s5[0], s5[1] = pack(partial)
    loop(1, HEAD, lambda step: to_head(*exchange5, step).start())
    r5[head] = s5[...]
    loop(1, HEAD, lambda step: from_head(*exchange5, step).wait_recv())
    attn = functools.reduce(jnp.add, [unpack(r5[peer, 0], r5[peer, 1]) for peer in range(HEAD)])
    s6[0], s6[1] = pack(attn)
    send_ctx(exchange6)
    r6[ctx] = s6[...]
    attn_ref[...] = attn
    gate_copy.wait()
    up_copy.wait()
    squares = jnp.zeros((ROWS, 512), F32)
    gate = jnp.zeros((ROWS, 256), F32)
    upper = jnp.zeros((ROWS, 256), F32)
    for step in [(0, 0)] + NEAREST:
        peer = other_ctx(step)
        if step != (0, 0):
            from_ctx(*exchange6, step).wait_recv()
        features = unpack(r6[peer, 0], r6[peer, 1])
        squares += features * features
        features = features[:, 0:COLS].astype(BF16)
        rows = pl.ds(pl.multiple_of(peer * COLS, COLS), COLS)
        gate += jnp.dot(features, w_gate[rows, :], preferred_element_type=F32)
        upper += jnp.dot(features, w_up[rows, :], preferred_element_type=F32)
    mean = jnp.sum(squares, axis=1, keepdims=True) * (1.0 / D)
    factor = 1.0 / jnp.sqrt(mean + 1e-06)
    gate = gate * factor
    upper = upper * factor
    hidden = (gate / (1.0 + jnp.exp(-gate)) * upper).astype(BF16)
    chosen = jnp.where(ids_ref[...] == ctx, gates_ref[...], 0.0)
    select = jnp.sum(chosen, axis=1, keepdims=True)
    down_copy.wait()
    result = jnp.dot(hidden, w_down[...], preferred_element_type=F32) * select
    for peer in range(CTX):
        left = peer * COLS // 128 * 128
        s7[peer, 0], s7[peer, 1] = pack(result[:, left : left + 512])
    send_ctx(exchange7)
    share = unpack(s7[ctx, 0], s7[ctx, 1])
    for step in NEAREST:
        peer = other_ctx(step)
        from_ctx(*exchange7, step).wait_recv()
        share += unpack(r7[peer, 0], r7[peer, 1])
    share = jnp.where(lax.rem(ctx, 2) == 1, pltpu.roll(share, 512 - COLS % 128, 1), share)
    for peer in range(HEAD):
        moved = share if peer == 0 else pltpu.roll(share, 512 - peer * OUT, 1)
        s8[peer] = moved[:, 0:128]
    loop(1, HEAD, lambda step: to_head(*exchange8, step).start())
    r8[head] = s8[head]
    loop(1, HEAD, lambda step: from_head(*exchange8, step).wait_recv())
    expert_ref[...] = functools.reduce(jnp.add, [r8[peer] for peer in range(HEAD)])

    query_copy.wait_send()
    loop(0, CHUNKS, lambda chunk: first_copy(chunk).wait_send())
    for exchange in (exchange3, exchange4, exchange6, exchange7):
        for step in NEAREST:
            to_ctx(*exchange, step).wait_send()

    def drain_head(step):
        to_head(*exchange5, step).wait_send()
        to_head(*exchange8, step).wait_send()

    loop(1, HEAD, drain_head)


def finish(attn_ref, expert_ref, attn_out_ref, expert_out_ref):
    attn_out_ref[...] = attn_ref[:, 0:COLS].astype(BF16)
    expert_out_ref[...] = expert_ref[:, 0:OUT].astype(BF16)


def body(
    q_nope,
    q_rope,
    latent_cache,
    lengths,
    w_key_absorb,
    w_value_up,
    w_output,
    w_gate,
    w_up,
    w_down,
    expert_ids,
    gate_weights,
):
    vmem = pl.BlockSpec(memory_space=pltpu.VMEM)
    hbm = pl.BlockSpec(memory_space=pl.ANY)
    dma = pltpu.SemaphoreType.DMA
    attn, expert = pl.pallas_call(
        kernel,
        out_shape=(
            jax.ShapeDtypeStruct((ROWS, 512), F32),
            jax.ShapeDtypeStruct((ROWS, 128), F32),
        ),
        in_specs=[pl.BlockSpec(memory_space=pltpu.SMEM)] + [vmem] * 4 + [hbm] * 7,
        out_specs=(vmem, vmem),
        scratch_shapes=[
            pltpu.VMEM((SLOTS, KEY, SPAN), BF16),
            pltpu.VMEM((GROUP, NOPE, LAT), BF16),
            pltpu.VMEM((GROUP, LAT, NOPE), BF16),
            pltpu.VMEM((512, GROUP * NOPE), BF16),
            pltpu.VMEM((D, 256), BF16),
            pltpu.VMEM((D, 256), BF16),
            pltpu.VMEM((256, D), BF16),
            pltpu.VMEM((ROWS, 2 * GROUP, KEY), BF16),
            pltpu.VMEM((CHUNKS, 2, TILES, 16, 128), BF16),
            pltpu.VMEM((CHUNKS, TILES, 16, 128), BF16),
            pltpu.VMEM((ROWS * GROUP, LAT), F32),
            pltpu.VMEM((ROWS * GROUP, 128), F32),
            pltpu.VMEM((EARLY + 1, 16, 128), BF16),
            pltpu.VMEM((CTX, EARLY + 1, 16, 128), BF16),
            pltpu.VMEM((LATE + 1, 16, 128), BF16),
            pltpu.VMEM((CTX, LATE + 1, 16, 128), BF16),
            pltpu.VMEM((ROWS * GROUP, NOPE), F32),
            pltpu.VMEM((2, 16, 128), BF16),
            pltpu.VMEM((HEAD, 2, 16, 128), BF16),
            pltpu.VMEM((2, 16, 128), BF16),
            pltpu.VMEM((CTX, 2, 16, 128), BF16),
            pltpu.VMEM((CTX, 2, 16, 128), BF16),
            pltpu.VMEM((CTX, 2, 16, 128), BF16),
            pltpu.VMEM((HEAD, ROWS, 128), F32),
            pltpu.VMEM((HEAD, ROWS, 128), F32),
            dma((ROWS,)),
            dma((6,)),
            dma((2,)),
            dma((CHUNKS,)),
            dma((CHUNKS,)),
            dma((CTX,)),
            dma((CTX,)),
            dma((CTX,)),
            dma((CTX,)),
            dma((HEAD,)),
            dma((HEAD,)),
            dma((CTX,)),
            dma((CTX,)),
            dma((CTX,)),
            dma((CTX,)),
            dma((HEAD,)),
            dma((HEAD,)),
        ],
        compiler_params=pltpu.CompilerParams(
            collective_id=0, has_side_effects=True, vmem_limit_bytes=60 * 2**20
        ),
    )(
        lengths,
        q_nope,
        q_rope,
        expert_ids,
        gate_weights,
        jnp.swapaxes(latent_cache, 1, 2),
        w_key_absorb,
        w_value_up,
        w_output.T,
        w_gate,
        w_up,
        w_down,
    )
    return pl.pallas_call(
        finish,
        out_shape=(
            jax.ShapeDtypeStruct((ROWS, COLS), BF16),
            jax.ShapeDtypeStruct((ROWS, OUT), BF16),
        ),
    )(attn, expert)


def solution(mesh):
    return jax.shard_map(
        body,
        mesh=mesh,
        in_specs=(
            P(None, "head", None),
            P(None, "head", None),
            P(None, "ctx", None),
            P(),
            P("head", None, None),
            P("head", None, None),
            P("head", "ctx"),
            P("ctx", None, "head"),
            P("ctx", None, "head"),
            P("ctx", "head", None),
            P(),
            P(),
        ),
        out_specs=(P(None, "ctx"), P(None, ("ctx", "head"))),
        check_vma=False,
    )
```

```python
import functools
import math

import jax
import jax.numpy as jnp
from jax import lax
from jax.experimental import pallas as pl
from jax.experimental.pallas import tpu as pltpu
from jax.sharding import PartitionSpec as P

ROWS = 8
HEADS = 128
NOPE = 128
ROPE = 64
LAT = 512
KEY = LAT + ROPE
D = 7168
CTX = 16
HEAD = 8
GROUP = HEADS // HEAD
SPAN = 8192 // 2
SLOTS = 6
COLS = D // CTX
OUT = COLS // HEAD
CHUNK = 2
CHUNKS = ROWS // CHUNK
TRANSPOSED = (((1,), (1,)), ((), ()))
TILES = CHUNK * 4 + 1
SCALE = (NOPE + ROPE) ** -0.5 * math.log2(math.e)
EARLY = 6
LATE = ROWS - EARLY
MESH = pl.DeviceIdType.MESH
F32 = jnp.float32
BF16 = jnp.bfloat16


def remote(src, dst, send_sem, recv_sem, device):
    return pltpu.make_async_remote_copy(
        src_ref=src,
        dst_ref=dst,
        send_sem=send_sem,
        recv_sem=recv_sem,
        device_id=device,
        device_id_type=MESH,
    )


def hops(step):
    return sum(min(part, 4 - part) for part in step)


NEAREST = sorted(((dy, dx) for dy in range(4) for dx in range(4) if dy or dx), key=hops)
FARTHEST = NEAREST[::-1]


def loop(low, high, step):
    def run(index, carry):
        step(index)
        return carry

    lax.fori_loop(low, high, run, 0)


def pack(wide):
    wide = wide.astype(BF16).astype(F32)
    first = jnp.concatenate([wide[:, 0:128], wide[:, 128:256]], axis=0).astype(BF16)
    second = jnp.concatenate([wide[:, 256:384], wide[:, 384:512]], axis=0).astype(BF16)
    return first, second


def unpack(first, second):
    first = first.astype(F32)
    second = second.astype(F32)
    return jnp.concatenate([first[0:8], first[8:16], second[0:8], second[8:16]], axis=1)


def split_three(value):
    high = value.astype(BF16).astype(F32)
    rest = value - high
    middle = rest.astype(BF16).astype(F32)
    return high, middle, rest - middle


def lanes(shape):
    return lax.broadcasted_iota(jnp.int32, shape, len(shape) - 1)


def put_levels(levels, rows):
    lane = lanes((rows, 128))
    tile = jnp.zeros((rows, 128), F32)
    for index, level in enumerate(levels):
        for part, value in enumerate(split_three(level)):
            tile = jnp.where(lane == 3 * index + part, value, tile)
    return tile


def get_level(tile, index):
    lane = lanes(tile.shape)
    wanted = (lane >= 3 * index) & (lane < 3 * index + 3)
    return jnp.sum(jnp.where(wanted, tile, 0.0), axis=1, keepdims=True)


def weights_of(levels):
    peak = functools.reduce(jnp.maximum, levels)
    parts = [jnp.exp2(level - peak) for level in levels]
    total = functools.reduce(jnp.add, parts)
    scale = 1.0 / total
    return [part * scale for part in parts], peak + jnp.log2(total)


def kernel(
    lengths_hbm,
    q_nope_hbm,
    q_rope_hbm,
    ids_hbm,
    gates_hbm,
    cache_hbm,
    absorb_hbm,
    value_hbm,
    output_hbm,
    gate_hbm,
    up_hbm,
    down_hbm,
    out_ref,
    lengths_ref,
    q_nope_ref,
    q_rope_ref,
    ids_ref,
    gates_ref,
    keys,
    absorb,
    value_up,
    w_out,
    w_gate,
    w_up,
    w_down,
    query,
    s1,
    r1,
    whole,
    whole_level,
    s3,
    r3,
    s4,
    r4,
    heads,
    s5,
    r5,
    s6,
    r6,
    s7,
    r7,
    s8,
    r8,
    key_sem,
    weight_sem,
    query_sem,
    s1_sem,
    r1_sem,
    s3_sem,
    r3_sem,
    s4_sem,
    r4_sem,
    s5_sem,
    r5_sem,
    s6_sem,
    r6_sem,
    s7_sem,
    r7_sem,
    s8_sem,
    r8_sem,
):
    ctx = lax.axis_index("ctx")
    head = lax.axis_index("head")
    core = lax.rem(head, 2)
    mate = {"head": head + 1 - 2 * core}

    def other_ctx(step):
        dy, dx = step
        return lax.rem(ctx // 4 + dy, 4) * 4 + lax.rem(lax.rem(ctx, 4) + dx, 4)

    def other_head(step):
        return lax.rem(head + step, HEAD)

    def key_copy(row):
        return pltpu.make_async_copy(
            cache_hbm.at[row, :, pl.ds(pl.multiple_of(core * SPAN, SPAN), SPAN)],
            keys.at[lax.rem(row, SLOTS)],
            key_sem.at[row],
        )

    absorb_copy = pltpu.make_async_copy(absorb_hbm, absorb, weight_sem.at[0])
    value_copy = pltpu.make_async_copy(value_hbm, value_up, weight_sem.at[1])
    output_copy = pltpu.make_async_copy(output_hbm, w_out.at[pl.ds(0, COLS)], weight_sem.at[2])
    gate_copy = pltpu.make_async_copy(gate_hbm.at[0], w_gate, weight_sem.at[3])
    up_copy = pltpu.make_async_copy(up_hbm.at[0], w_up, weight_sem.at[4])
    down_copy = pltpu.make_async_copy(down_hbm.at[0], w_down, weight_sem.at[5])
    small_copies = [
        pltpu.make_async_copy(src, dst, weight_sem.at[6 + index])
        for index, (src, dst) in enumerate(
            (
                (q_nope_hbm, q_nope_ref),
                (q_rope_hbm, q_rope_ref),
                (lengths_hbm, lengths_ref),
                (ids_hbm, ids_ref),
                (gates_hbm, gates_ref),
            )
        )
    ]
    small_copies[0].start()
    absorb_copy.start()
    for copy in small_copies[1:]:
        copy.start()
    loop(0, 2, lambda row: key_copy(row).start())
    barrier = pltpu.get_barrier_semaphore()

    def greet(device):
        pl.semaphore_signal(barrier, inc=1, device_id=device, device_id_type=MESH)

    for step in FARTHEST:
        greet({"ctx": other_ctx(step)})
    loop(1, HEAD, lambda step: greet({"head": other_head(step)}))
    loop(2, SLOTS, lambda row: key_copy(row).start())
    value_copy.start()
    output_copy.start()

    w_out[pl.ds(COLS, 512 - COLS), :] = jnp.zeros((512 - COLS, GROUP * NOPE), BF16)
    small_copies[0].wait()
    flat = q_nope_ref[...].reshape(ROWS * GROUP, NOPE).astype(F32)
    which = lax.rem(lax.broadcasted_iota(jnp.int32, (ROWS * GROUP, NOPE), 0), GROUP)
    blocks = [jnp.where(which == h, flat, 0.0).astype(BF16) for h in range(GROUP)]
    wide_query = jnp.concatenate(blocks, axis=1)
    absorb_copy.wait()
    latent = jnp.dot(
        wide_query,
        absorb[...].reshape(GROUP * NOPE, LAT),
        preferred_element_type=F32,
    ).astype(BF16)
    mine = pl.ds(pl.multiple_of(core * GROUP, GROUP), GROUP)
    query[:, mine, 0:LAT] = latent.reshape(ROWS, GROUP, LAT)
    small_copies[1].wait()
    query[:, mine, LAT:KEY] = q_rope_ref[...]
    pl.semaphore_wait(barrier, HEAD - 1 + CTX - 1)
    query_copy = remote(
        query.at[:, mine], query.at[:, mine], query_sem.at[0], query_sem.at[1], mate
    )
    query_copy.start()
    query_copy.wait_recv()

    for copy in small_copies[2:]:
        copy.wait()
    position = ctx * (2 * SPAN) + core * SPAN + lanes((1, SPAN))

    def attend_row(row):
        block = keys.at[lax.rem(row, SLOTS)]
        score = jnp.dot(query[row], block[...], preferred_element_type=F32)
        score = jnp.where(position < lengths_ref[row], score, -1e30)
        peak = jnp.max(score, axis=1, keepdims=True)
        weight = jnp.exp2((score - peak) * SCALE)
        total = jnp.sum(weight, axis=1, keepdims=True)
        summed = lax.dot_general(
            block[0:LAT], weight.astype(BF16), TRANSPOSED, preferred_element_type=F32
        )
        return summed.T * (1.0 / total), peak * SCALE + jnp.log2(total)

    def first_copy(chunk):
        return remote(
            s1.at[chunk, 1 - core], r1.at[chunk], s1_sem.at[chunk], r1_sem.at[chunk], mate
        )

    def attend(chunk):
        for row in range(CHUNK):
            key_copy(chunk * CHUNK + row).wait()
        results = [attend_row(chunk * CHUNK + row) for row in range(CHUNK)]
        level = put_levels([result[1] for result in results], 2 * GROUP)
        for group in range(2):
            rows = slice(group * GROUP, (group + 1) * GROUP)
            for row in range(CHUNK):
                for tile in range(4):
                    s1[chunk, group, row * 4 + tile] = results[row][0][
                        rows, tile * 128 : (tile + 1) * 128
                    ].astype(BF16)
            s1[chunk, group, CHUNK * 4] = level[rows].astype(BF16)
        first_copy(chunk).start()

    def merge_cores(chunk):
        first_copy(chunk).wait_recv()
        blocks = [s1.at[chunk, core], r1.at[chunk]]
        tiles = [block[CHUNK * 4].astype(F32) for block in blocks]
        for row in range(CHUNK):
            parts, level = weights_of([get_level(tile, row) for tile in tiles])
            rows = pl.ds(pl.multiple_of((chunk * CHUNK + row) * GROUP, GROUP), GROUP)
            for tile in range(4):
                whole[rows, tile * 128 : (tile + 1) * 128] = functools.reduce(
                    jnp.add,
                    [
                        block[row * 4 + tile].astype(F32) * part
                        for block, part in zip(blocks, parts)
                    ],
                )
            whole_level[rows, :] = jnp.broadcast_to(level, (GROUP, 128))

    def to_ctx(src, dst, send_sem, recv_sem, step):
        peer = other_ctx(step)
        return remote(src(peer), dst.at[ctx], send_sem.at[peer], recv_sem.at[ctx], {"ctx": peer})

    def from_ctx(src, dst, send_sem, recv_sem, step):
        peer = other_ctx(step)
        return remote(src(peer), dst.at[peer], send_sem.at[peer], recv_sem.at[peer], {"ctx": peer})

    def to_head(src, dst, send_sem, recv_sem, step):
        peer = other_head(step)
        return remote(src(peer), dst.at[head], send_sem.at[peer], recv_sem.at[head], {"head": peer})

    def from_head(src, dst, send_sem, recv_sem, step):
        peer = other_head(step)
        return remote(src(peer), dst.at[peer], send_sem.at[peer], recv_sem.at[peer], {"head": peer})

    exchange3 = (lambda peer: s3, r3, s3_sem, r3_sem)
    exchange4 = (lambda peer: s4, r4, s4_sem, r4_sem)
    exchange5 = (lambda peer: s5, r5, s5_sem, r5_sem)
    exchange6 = (lambda peer: s6, r6, s6_sem, r6_sem)
    exchange7 = (lambda peer: s7.at[peer], r7, s7_sem, r7_sem)
    exchange8 = (lambda peer: s8.at[peer], r8, s8_sem, r8_sem)

    def send_ctx(exchange):
        for step in FARTHEST:
            to_ctx(*exchange, step).start()

    def receive_ctx(exchange):
        for step in NEAREST:
            from_ctx(*exchange, step).wait_recv()

    def project(first, count, exchange):
        rows = pl.ds(first * GROUP, count * GROUP)
        merged = whole[rows, :]
        which = lax.rem(lax.broadcasted_iota(jnp.int32, (count * GROUP, LAT), 0), GROUP)
        blocks = [jnp.where(which == h, merged, 0.0).astype(BF16) for h in range(GROUP)]
        share = jnp.dot(
            jnp.concatenate(blocks, axis=1),
            value_up[...].reshape(GROUP * LAT, NOPE),
            preferred_element_type=F32,
        ).astype(BF16)
        src = exchange[0](0)
        src[0:count] = share.reshape(count, GROUP, NOPE)
        levels = [whole_level[pl.ds((first + row) * GROUP, GROUP), :] for row in range(count)]
        src[count] = put_levels(levels, GROUP).astype(BF16)
        send_ctx(exchange)
        exchange[1][ctx] = src[...]

    def merge_ctx(first, count, exchange):
        receive_ctx(exchange)
        arrived = exchange[1]
        tiles = [arrived[peer, count].astype(F32) for peer in range(CTX)]
        for row in range(count):
            parts, _ = weights_of([get_level(tile, row) for tile in tiles])
            heads[pl.ds((first + row) * GROUP, GROUP), :] = functools.reduce(
                jnp.add, [arrived[peer, row].astype(F32) * parts[peer] for peer in range(CTX)]
            )

    def stage(chunk):
        attend(chunk)

        @pl.when(chunk == 0)
        def _():
            loop(SLOTS, ROWS, lambda row: key_copy(row).start())
            gate_copy.start()
            up_copy.start()
            down_copy.start()

        @pl.when(chunk >= 1)
        def _():
            merge_cores(chunk - 1)

    loop(0, CHUNKS - 1, stage)
    merge_cores(CHUNKS - 2)
    value_copy.wait()
    project(0, EARLY, exchange3)
    attend(CHUNKS - 1)
    merge_cores(CHUNKS - 1)
    project(EARLY, LATE, exchange4)
    merge_ctx(0, EARLY, exchange3)
    output_copy.wait()
    merge_ctx(EARLY, LATE, exchange4)
    gathered = [heads[pl.ds(member, ROWS, stride=GROUP), :] for member in range(GROUP)]
    partial = lax.dot_general(
        jnp.concatenate(gathered, axis=1).astype(BF16),
        w_out[...],
        TRANSPOSED,
        preferred_element_type=F32,
    )
    s5[0], s5[1] = pack(partial)
    loop(1, HEAD, lambda step: to_head(*exchange5, step).start())
    r5[head] = s5[...]
    query_copy.wait_send()
    loop(0, CHUNKS, lambda chunk: first_copy(chunk).wait_send())
    for exchange in (exchange3, exchange4):
        for step in NEAREST:
            to_ctx(*exchange, step).wait_send()
    loop(1, HEAD, lambda step: from_head(*exchange5, step).wait_recv())
    attn = functools.reduce(jnp.add, [unpack(r5[peer, 0], r5[peer, 1]) for peer in range(HEAD)])
    s6[0], s6[1] = pack(attn)
    send_ctx(exchange6)
    r6[ctx] = s6[...]
    out_ref[:, 0:512] = attn
    gate_copy.wait()
    up_copy.wait()
    squares = jnp.zeros((ROWS, 512), F32)
    gate = jnp.zeros((ROWS, 256), F32)
    upper = jnp.zeros((ROWS, 256), F32)
    for step in [(0, 0)] + NEAREST:
        peer = other_ctx(step)
        if step != (0, 0):
            from_ctx(*exchange6, step).wait_recv()
        features = unpack(r6[peer, 0], r6[peer, 1])
        squares += features * features
        features = features[:, 0:COLS].astype(BF16)
        rows = pl.ds(pl.multiple_of(peer * COLS, COLS), COLS)
        gate += jnp.dot(features, w_gate[rows, :], preferred_element_type=F32)
        upper += jnp.dot(features, w_up[rows, :], preferred_element_type=F32)
    mean = jnp.sum(squares, axis=1, keepdims=True) * (1.0 / D)
    factor = 1.0 / jnp.sqrt(mean + 1e-06)
    gate = gate * factor
    upper = upper * factor
    hidden = (gate / (1.0 + jnp.exp(-gate)) * upper).astype(BF16)
    chosen = jnp.where(ids_ref[...] == ctx, gates_ref[...], 0.0)
    select = jnp.sum(chosen, axis=1, keepdims=True)
    down_copy.wait()
    result = jnp.dot(hidden, w_down[...], preferred_element_type=F32) * select
    for peer in range(CTX):
        left = peer * COLS // 128 * 128
        s7[peer, 0], s7[peer, 1] = pack(result[:, left : left + 512])
    send_ctx(exchange7)
    share = unpack(s7[ctx, 0], s7[ctx, 1])
    for step in NEAREST:
        peer = other_ctx(step)
        from_ctx(*exchange7, step).wait_recv()
        share += unpack(r7[peer, 0], r7[peer, 1])
    share = jnp.where(lax.rem(ctx, 2) == 1, pltpu.roll(share, 512 - COLS % 128, 1), share)
    for peer in range(HEAD):
        moved = share if peer == 0 else pltpu.roll(share, 512 - peer * OUT, 1)
        s8[peer] = moved[:, 0:128]
    loop(1, HEAD, lambda step: to_head(*exchange8, step).start())
    r8[head] = s8[head]
    for step in NEAREST:
        to_ctx(*exchange6, step).wait_send()
    loop(1, HEAD, lambda step: to_head(*exchange5, step).wait_send())
    loop(1, HEAD, lambda step: from_head(*exchange8, step).wait_recv())
    out_ref[:, 512:640] = functools.reduce(jnp.add, [r8[peer] for peer in range(HEAD)])

    for step in NEAREST:
        to_ctx(*exchange7, step).wait_send()
    loop(1, HEAD, lambda step: to_head(*exchange8, step).wait_send())


def finish(both_ref, attn_ref, expert_ref):
    attn_ref[...] = both_ref[:, 0:COLS].astype(BF16)
    expert_ref[...] = both_ref[:, 512 : 512 + OUT].astype(BF16)


def body(
    q_nope,
    q_rope,
    latent_cache,
    lengths,
    w_key_absorb,
    w_value_up,
    w_output,
    w_gate,
    w_up,
    w_down,
    expert_ids,
    gate_weights,
):
    vmem = pl.BlockSpec(memory_space=pltpu.VMEM)
    hbm = pl.BlockSpec(memory_space=pl.ANY)
    dma = pltpu.SemaphoreType.DMA
    both = pl.pallas_call(
        kernel,
        out_shape=pltpu.VMEM((ROWS, 640), F32),
        in_specs=[hbm] * 12,
        out_specs=vmem,
        scratch_shapes=[
            pltpu.SMEM((ROWS,), jnp.int32),
            pltpu.VMEM((ROWS, GROUP, NOPE), BF16),
            pltpu.VMEM((ROWS, GROUP, ROPE), BF16),
            pltpu.VMEM((ROWS, 8), jnp.int32),
            pltpu.VMEM((ROWS, 8), F32),
            pltpu.VMEM((SLOTS, KEY, SPAN), BF16),
            pltpu.VMEM((GROUP, NOPE, LAT), BF16),
            pltpu.VMEM((GROUP, LAT, NOPE), BF16),
            pltpu.VMEM((512, GROUP * NOPE), BF16),
            pltpu.VMEM((D, 256), BF16),
            pltpu.VMEM((D, 256), BF16),
            pltpu.VMEM((256, D), BF16),
            pltpu.VMEM((ROWS, 2 * GROUP, KEY), BF16),
            pltpu.VMEM((CHUNKS, 2, TILES, 16, 128), BF16),
            pltpu.VMEM((CHUNKS, TILES, 16, 128), BF16),
            pltpu.VMEM((ROWS * GROUP, LAT), F32),
            pltpu.VMEM((ROWS * GROUP, 128), F32),
            pltpu.VMEM((EARLY + 1, 16, 128), BF16),
            pltpu.VMEM((CTX, EARLY + 1, 16, 128), BF16),
            pltpu.VMEM((LATE + 1, 16, 128), BF16),
            pltpu.VMEM((CTX, LATE + 1, 16, 128), BF16),
            pltpu.VMEM((ROWS * GROUP, NOPE), F32),
            pltpu.VMEM((2, 16, 128), BF16),
            pltpu.VMEM((HEAD, 2, 16, 128), BF16),
            pltpu.VMEM((2, 16, 128), BF16),
            pltpu.VMEM((CTX, 2, 16, 128), BF16),
            pltpu.VMEM((CTX, 2, 16, 128), BF16),
            pltpu.VMEM((CTX, 2, 16, 128), BF16),
            pltpu.VMEM((HEAD, ROWS, 128), F32),
            pltpu.VMEM((HEAD, ROWS, 128), F32),
            dma((ROWS,)),
            dma((11,)),
            dma((2,)),
            dma((CHUNKS,)),
            dma((CHUNKS,)),
            dma((CTX,)),
            dma((CTX,)),
            dma((CTX,)),
            dma((CTX,)),
            dma((HEAD,)),
            dma((HEAD,)),
            dma((CTX,)),
            dma((CTX,)),
            dma((CTX,)),
            dma((CTX,)),
            dma((HEAD,)),
            dma((HEAD,)),
        ],
        compiler_params=pltpu.CompilerParams(
            collective_id=0, has_side_effects=True, vmem_limit_bytes=60 * 2**20
        ),
    )(
        lengths,
        q_nope,
        q_rope,
        expert_ids,
        gate_weights,
        jnp.swapaxes(latent_cache, 1, 2),
        w_key_absorb,
        w_value_up,
        w_output.T,
        w_gate,
        w_up,
        w_down,
    )
    return pl.pallas_call(
        finish,
        out_shape=(
            jax.ShapeDtypeStruct((ROWS, COLS), BF16),
            jax.ShapeDtypeStruct((ROWS, OUT), BF16),
        ),
    )(both)


def solution(mesh):
    return jax.shard_map(
        body,
        mesh=mesh,
        in_specs=(
            P(None, "head", None),
            P(None, "head", None),
            P(None, "ctx", None),
            P(),
            P("head", None, None),
            P("head", None, None),
            P("head", "ctx"),
            P("ctx", None, "head"),
            P("ctx", None, "head"),
            P("ctx", "head", None),
            P(),
            P(),
        ),
        out_specs=(P(None, "ctx"), P(None, ("ctx", "head"))),
        check_vma=False,
    )
```

```python
import functools
import math

import jax
import jax.numpy as jnp
from jax import lax
from jax.experimental import pallas as pl
from jax.experimental.pallas import tpu as pltpu
from jax.sharding import PartitionSpec as P

ROWS = 8
HEADS = 128
NOPE = 128
ROPE = 64
LAT = 512
KEY = LAT + ROPE
D = 7168
CTX = 16
HEAD = 8
GROUP = HEADS // HEAD
SPAN = 8192 // 2
SLOTS = 6
COLS = D // CTX
OUT = COLS // HEAD
CHUNK = 2
CHUNKS = ROWS // CHUNK
TILES = CHUNK * 4 + 1
SCALE = (NOPE + ROPE) ** -0.5 * math.log2(math.e)
EARLY = 6
LATE = ROWS - EARLY
MESH = pl.DeviceIdType.MESH
F32 = jnp.float32
BF16 = jnp.bfloat16


def remote(src, dst, send_sem, recv_sem, device):
    return pltpu.make_async_remote_copy(
        src_ref=src,
        dst_ref=dst,
        send_sem=send_sem,
        recv_sem=recv_sem,
        device_id=device,
        device_id_type=MESH,
    )


def hops(step):
    return sum(min(part, 4 - part) for part in step)


NEAREST = sorted(((dy, dx) for dy in range(4) for dx in range(4) if dy or dx), key=hops)
FARTHEST = NEAREST[::-1]


def loop(low, high, step):
    def run(index, carry):
        step(index)
        return carry

    lax.fori_loop(low, high, run, 0)


def pack(wide):
    wide = wide.astype(BF16).astype(F32)
    first = jnp.concatenate([wide[:, 0:128], wide[:, 128:256]], axis=0).astype(BF16)
    second = jnp.concatenate([wide[:, 256:384], wide[:, 384:512]], axis=0).astype(BF16)
    return first, second


def unpack(first, second):
    first = first.astype(F32)
    second = second.astype(F32)
    return jnp.concatenate([first[0:8], first[8:16], second[0:8], second[8:16]], axis=1)


def split_three(value):
    high = value.astype(BF16).astype(F32)
    rest = value - high
    middle = rest.astype(BF16).astype(F32)
    return high, middle, rest - middle


def lanes(shape):
    return lax.broadcasted_iota(jnp.int32, shape, len(shape) - 1)


def put_levels(levels, rows):
    lane = lanes((rows, 128))
    tile = jnp.zeros((rows, 128), F32)
    for index, level in enumerate(levels):
        for part, value in enumerate(split_three(level)):
            tile = jnp.where(lane == 3 * index + part, value, tile)
    return tile


def get_level(tile, index):
    lane = lanes(tile.shape)
    wanted = (lane >= 3 * index) & (lane < 3 * index + 3)
    return jnp.sum(jnp.where(wanted, tile, 0.0), axis=1, keepdims=True)


def weights_of(levels):
    peak = functools.reduce(jnp.maximum, levels)
    parts = [jnp.exp2(level - peak) for level in levels]
    total = functools.reduce(jnp.add, parts)
    scale = 1.0 / total
    return [part * scale for part in parts], peak + jnp.log2(total)


def kernel(
    lengths_hbm,
    q_nope_hbm,
    q_rope_hbm,
    ids_hbm,
    gates_hbm,
    cache_hbm,
    absorb_hbm,
    value_hbm,
    output_hbm,
    gate_hbm,
    up_hbm,
    down_hbm,
    out_ref,
    lengths_ref,
    q_nope_ref,
    q_rope_ref,
    ids_ref,
    gates_ref,
    keys,
    values_a,
    values_b,
    absorb,
    value_up,
    w_out,
    w_gate,
    w_up,
    w_down,
    query,
    s1,
    r1,
    whole,
    whole_level,
    s3,
    r3,
    s4,
    r4,
    heads,
    s5,
    r5,
    s6,
    r6,
    s7,
    r7,
    s8,
    r8,
    key_sem,
    weight_sem,
    query_sem,
    s1_sem,
    r1_sem,
    s3_sem,
    r3_sem,
    s4_sem,
    r4_sem,
    s5_sem,
    r5_sem,
    s6_sem,
    r6_sem,
    s7_sem,
    r7_sem,
    s8_sem,
    r8_sem,
):
    ctx = lax.axis_index("ctx")
    head = lax.axis_index("head")
    core = lax.rem(head, 2)
    mate = {"head": head + 1 - 2 * core}

    def other_ctx(step):
        dy, dx = step
        return lax.rem(ctx // 4 + dy, 4) * 4 + lax.rem(lax.rem(ctx, 4) + dx, 4)

    def other_head(step):
        return lax.rem(head + step, HEAD)

    def key_copy(row):
        return pltpu.make_async_copy(
            cache_hbm.at[row, :, pl.ds(pl.multiple_of(core * SPAN, SPAN), SPAN)],
            keys.at[lax.rem(row, SLOTS)],
            key_sem.at[row],
        )

    absorb_copy = pltpu.make_async_copy(absorb_hbm, absorb, weight_sem.at[0])
    value_copy = pltpu.make_async_copy(value_hbm, value_up, weight_sem.at[1])
    output_copy = pltpu.make_async_copy(output_hbm, w_out.at[pl.ds(0, COLS)], weight_sem.at[2])
    gate_copy = pltpu.make_async_copy(gate_hbm.at[0], w_gate, weight_sem.at[3])
    up_copy = pltpu.make_async_copy(up_hbm.at[0], w_up, weight_sem.at[4])
    down_copy = pltpu.make_async_copy(down_hbm.at[0], w_down, weight_sem.at[5])
    small_copies = [
        pltpu.make_async_copy(src, dst, weight_sem.at[6 + index])
        for index, (src, dst) in enumerate(
            (
                (q_nope_hbm, q_nope_ref),
                (q_rope_hbm, q_rope_ref),
                (lengths_hbm, lengths_ref),
                (ids_hbm, ids_ref),
                (gates_hbm, gates_ref),
            )
        )
    ]
    small_copies[0].start()
    absorb_copy.start()
    for copy in small_copies[1:]:
        copy.start()
    loop(0, 2, lambda row: key_copy(row).start())
    barrier = pltpu.get_barrier_semaphore()

    def greet(device):
        pl.semaphore_signal(barrier, inc=1, device_id=device, device_id_type=MESH)

    for step in FARTHEST:
        greet({"ctx": other_ctx(step)})
    loop(1, HEAD, lambda step: greet({"head": other_head(step)}))
    loop(2, SLOTS, lambda row: key_copy(row).start())
    value_copy.start()
    output_copy.start()

    w_out[pl.ds(COLS, 512 - COLS), :] = jnp.zeros((512 - COLS, GROUP * NOPE), BF16)
    small_copies[0].wait()
    flat = q_nope_ref[...].reshape(ROWS * GROUP, NOPE).astype(F32)
    which = lax.rem(lax.broadcasted_iota(jnp.int32, (ROWS * GROUP, NOPE), 0), GROUP)
    blocks = [jnp.where(which == h, flat, 0.0).astype(BF16) for h in range(GROUP)]
    wide_query = jnp.concatenate(blocks, axis=1)
    absorb_copy.wait()
    latent = jnp.dot(
        wide_query,
        absorb[...].reshape(GROUP * NOPE, LAT),
        preferred_element_type=F32,
    ).astype(BF16)
    mine = pl.ds(pl.multiple_of(core * GROUP, GROUP), GROUP)
    query[:, mine, 0:LAT] = latent.reshape(ROWS, GROUP, LAT)
    small_copies[1].wait()
    query[:, mine, LAT:KEY] = q_rope_ref[...]
    pl.semaphore_wait(barrier, HEAD - 1 + CTX - 1)
    query_copy = remote(
        query.at[:, mine], query.at[:, mine], query_sem.at[0], query_sem.at[1], mate
    )
    query_copy.start()
    for copy in small_copies[2:]:
        copy.wait()
    position = ctx * (2 * SPAN) + core * SPAN + lanes((1, SPAN))

    def slot(row):
        return keys.at[lax.rem(row, SLOTS)]

    def scores(row):
        score = jnp.dot(query[row], slot(row)[...], preferred_element_type=F32)
        return jnp.where(position < lengths_ref[row], score, -1e30)

    def soften(score):
        peak = jnp.max(score, axis=1, keepdims=True)
        weight = jnp.exp2((score - peak) * SCALE)
        total = jnp.sum(weight, axis=1, keepdims=True)
        return weight.astype(BF16), 1.0 / total, peak * SCALE + jnp.log2(total)

    def turn(row, values):
        values[...] = slot(row)[0:LAT, :].T

    key_copy(0).wait()
    turn(0, values_a)
    query_copy.wait_recv()

    def attend_pair(first, more):
        key_copy(first + 1).wait()
        if more:
            key_copy(first + 2).wait()
        score = scores(first)
        turn(first + 1, values_b)
        weight, inverse, level_a = soften(score)
        score = scores(first + 1)
        summed_a = jnp.dot(weight, values_a[...], preferred_element_type=F32) * inverse
        if more:
            turn(first + 2, values_a)
        weight, inverse, level_b = soften(score)
        summed_b = jnp.dot(weight, values_b[...], preferred_element_type=F32) * inverse
        return (summed_a, level_a), (summed_b, level_b)

    def first_copy(chunk):
        return remote(
            s1.at[chunk, 1 - core], r1.at[chunk], s1_sem.at[chunk], r1_sem.at[chunk], mate
        )

    def attend(chunk, more):
        results = attend_pair(chunk * CHUNK, more)
        level = put_levels([result[1] for result in results], 2 * GROUP)
        for group in range(2):
            rows = slice(group * GROUP, (group + 1) * GROUP)
            for row in range(CHUNK):
                for tile in range(4):
                    s1[chunk, group, row * 4 + tile] = results[row][0][
                        rows, tile * 128 : (tile + 1) * 128
                    ].astype(BF16)
            s1[chunk, group, CHUNK * 4] = level[rows].astype(BF16)
        first_copy(chunk).start()

    def merge_cores(chunk):
        first_copy(chunk).wait_recv()
        blocks = [s1.at[chunk, core], r1.at[chunk]]
        tiles = [block[CHUNK * 4].astype(F32) for block in blocks]
        for row in range(CHUNK):
            parts, level = weights_of([get_level(tile, row) for tile in tiles])
            rows = pl.ds(pl.multiple_of((chunk * CHUNK + row) * GROUP, GROUP), GROUP)
            for tile in range(4):
                whole[rows, tile * 128 : (tile + 1) * 128] = functools.reduce(
                    jnp.add,
                    [
                        block[row * 4 + tile].astype(F32) * part
                        for block, part in zip(blocks, parts)
                    ],
                )
            whole_level[rows, :] = jnp.broadcast_to(level, (GROUP, 128))

    def to_ctx(src, dst, send_sem, recv_sem, step):
        peer = other_ctx(step)
        return remote(src(peer), dst.at[ctx], send_sem.at[peer], recv_sem.at[ctx], {"ctx": peer})

    def from_ctx(src, dst, send_sem, recv_sem, step):
        peer = other_ctx(step)
        return remote(src(peer), dst.at[peer], send_sem.at[peer], recv_sem.at[peer], {"ctx": peer})

    def to_head(src, dst, send_sem, recv_sem, step):
        peer = other_head(step)
        return remote(src(peer), dst.at[head], send_sem.at[peer], recv_sem.at[head], {"head": peer})

    def from_head(src, dst, send_sem, recv_sem, step):
        peer = other_head(step)
        return remote(src(peer), dst.at[peer], send_sem.at[peer], recv_sem.at[peer], {"head": peer})

    exchange3 = (lambda peer: s3, r3, s3_sem, r3_sem)
    exchange4 = (lambda peer: s4, r4, s4_sem, r4_sem)
    exchange5 = (lambda peer: s5, r5, s5_sem, r5_sem)
    exchange6 = (lambda peer: s6, r6, s6_sem, r6_sem)
    exchange7 = (lambda peer: s7.at[peer], r7, s7_sem, r7_sem)
    exchange8 = (lambda peer: s8.at[peer], r8, s8_sem, r8_sem)

    def send_ctx(exchange):
        for step in FARTHEST:
            to_ctx(*exchange, step).start()

    def receive_ctx(exchange):
        for step in NEAREST:
            from_ctx(*exchange, step).wait_recv()

    def project(first, count, exchange):
        rows = pl.ds(first * GROUP, count * GROUP)
        merged = whole[rows, :]
        which = lax.rem(lax.broadcasted_iota(jnp.int32, (count * GROUP, LAT), 0), GROUP)
        blocks = [jnp.where(which == h, merged, 0.0).astype(BF16) for h in range(GROUP)]
        share = jnp.dot(
            jnp.concatenate(blocks, axis=1),
            value_up[...].reshape(GROUP * LAT, NOPE),
            preferred_element_type=F32,
        ).astype(BF16)
        src = exchange[0](0)
        src[0:count] = share.reshape(count, GROUP, NOPE)
        levels = [whole_level[pl.ds((first + row) * GROUP, GROUP), :] for row in range(count)]
        src[count] = put_levels(levels, GROUP).astype(BF16)
        send_ctx(exchange)
        exchange[1][ctx] = src[...]

    def merge_ctx(first, count, exchange):
        receive_ctx(exchange)
        arrived = exchange[1]
        tiles = [arrived[peer, count].astype(F32) for peer in range(CTX)]
        for row in range(count):
            parts, _ = weights_of([get_level(tile, row) for tile in tiles])
            heads[pl.ds((first + row) * GROUP, GROUP), :] = functools.reduce(
                jnp.add, [arrived[peer, row].astype(F32) * parts[peer] for peer in range(CTX)]
            )

    def stage(chunk):
        attend(chunk, True)

        @pl.when(chunk == 0)
        def _():
            loop(SLOTS, ROWS, lambda row: key_copy(row).start())
            gate_copy.start()
            up_copy.start()
            down_copy.start()

        @pl.when(chunk >= 1)
        def _():
            merge_cores(chunk - 1)

    loop(0, CHUNKS - 1, stage)
    merge_cores(CHUNKS - 2)
    value_copy.wait()
    project(0, EARLY, exchange3)
    attend(CHUNKS - 1, False)
    merge_cores(CHUNKS - 1)
    project(EARLY, LATE, exchange4)
    output_copy.wait()
    values_a[0 : GROUP * NOPE, :] = w_out[...].T
    merge_ctx(0, EARLY, exchange3)
    merge_ctx(EARLY, LATE, exchange4)
    gathered = [heads[pl.ds(member, ROWS, stride=GROUP), :] for member in range(GROUP)]
    partial = jnp.dot(
        jnp.concatenate(gathered, axis=1).astype(BF16),
        values_a[0 : GROUP * NOPE, :],
        preferred_element_type=F32,
    )
    s5[0], s5[1] = pack(partial)
    loop(1, HEAD, lambda step: to_head(*exchange5, step).start())
    r5[head] = s5[...]
    query_copy.wait_send()
    loop(0, CHUNKS, lambda chunk: first_copy(chunk).wait_send())
    for exchange in (exchange3, exchange4):
        for step in NEAREST:
            to_ctx(*exchange, step).wait_send()
    loop(1, HEAD, lambda step: from_head(*exchange5, step).wait_recv())
    attn = functools.reduce(jnp.add, [unpack(r5[peer, 0], r5[peer, 1]) for peer in range(HEAD)])
    s6[0], s6[1] = pack(attn)
    send_ctx(exchange6)
    r6[ctx] = s6[...]
    out_ref[:, 0:512] = attn
    gate_copy.wait()
    up_copy.wait()
    squares = jnp.zeros((ROWS, 512), F32)
    gate = jnp.zeros((ROWS, 256), F32)
    upper = jnp.zeros((ROWS, 256), F32)
    for step in [(0, 0)] + NEAREST:
        peer = other_ctx(step)
        if step != (0, 0):
            from_ctx(*exchange6, step).wait_recv()
        features = unpack(r6[peer, 0], r6[peer, 1])
        squares += features * features
        features = features[:, 0:COLS].astype(BF16)
        rows = pl.ds(pl.multiple_of(peer * COLS, COLS), COLS)
        gate += jnp.dot(features, w_gate[rows, :], preferred_element_type=F32)
        upper += jnp.dot(features, w_up[rows, :], preferred_element_type=F32)
    mean = jnp.sum(squares, axis=1, keepdims=True) * (1.0 / D)
    factor = 1.0 / jnp.sqrt(mean + 1e-06)
    gate = gate * factor
    upper = upper * factor
    hidden = (gate / (1.0 + jnp.exp(-gate)) * upper).astype(BF16)
    chosen = jnp.where(ids_ref[...] == ctx, gates_ref[...], 0.0)
    select = jnp.sum(chosen, axis=1, keepdims=True)
    down_copy.wait()
    result = jnp.dot(hidden, w_down[...], preferred_element_type=F32) * select
    for peer in range(CTX):
        left = peer * COLS // 128 * 128
        s7[peer, 0], s7[peer, 1] = pack(result[:, left : left + 512])
    send_ctx(exchange7)
    share = unpack(s7[ctx, 0], s7[ctx, 1])
    for step in NEAREST:
        peer = other_ctx(step)
        from_ctx(*exchange7, step).wait_recv()
        share += unpack(r7[peer, 0], r7[peer, 1])
    share = jnp.where(lax.rem(ctx, 2) == 1, pltpu.roll(share, 512 - COLS % 128, 1), share)
    for peer in range(HEAD):
        moved = share if peer == 0 else pltpu.roll(share, 512 - peer * OUT, 1)
        s8[peer] = moved[:, 0:128]
    loop(1, HEAD, lambda step: to_head(*exchange8, step).start())
    r8[head] = s8[head]
    for step in NEAREST:
        to_ctx(*exchange6, step).wait_send()
    loop(1, HEAD, lambda step: to_head(*exchange5, step).wait_send())
    loop(1, HEAD, lambda step: from_head(*exchange8, step).wait_recv())
    out_ref[:, 512:640] = functools.reduce(jnp.add, [r8[peer] for peer in range(HEAD)])

    for step in NEAREST:
        to_ctx(*exchange7, step).wait_send()
    loop(1, HEAD, lambda step: to_head(*exchange8, step).wait_send())


def finish(both_ref, attn_ref, expert_ref):
    attn_ref[...] = both_ref[:, 0:COLS].astype(BF16)
    expert_ref[...] = both_ref[:, 512 : 512 + OUT].astype(BF16)


def body(
    q_nope,
    q_rope,
    latent_cache,
    lengths,
    w_key_absorb,
    w_value_up,
    w_output,
    w_gate,
    w_up,
    w_down,
    expert_ids,
    gate_weights,
):
    vmem = pl.BlockSpec(memory_space=pltpu.VMEM)
    hbm = pl.BlockSpec(memory_space=pl.ANY)
    dma = pltpu.SemaphoreType.DMA
    both = pl.pallas_call(
        kernel,
        out_shape=pltpu.VMEM((ROWS, 640), F32),
        in_specs=[hbm] * 12,
        out_specs=vmem,
        scratch_shapes=[
            pltpu.SMEM((ROWS,), jnp.int32),
            pltpu.VMEM((ROWS, GROUP, NOPE), BF16),
            pltpu.VMEM((ROWS, GROUP, ROPE), BF16),
            pltpu.VMEM((ROWS, 8), jnp.int32),
            pltpu.VMEM((ROWS, 8), F32),
            pltpu.VMEM((SLOTS, KEY, SPAN), BF16),
            pltpu.VMEM((SPAN, LAT), BF16),
            pltpu.VMEM((SPAN, LAT), BF16),
            pltpu.VMEM((GROUP, NOPE, LAT), BF16),
            pltpu.VMEM((GROUP, LAT, NOPE), BF16),
            pltpu.VMEM((512, GROUP * NOPE), BF16),
            pltpu.VMEM((D, 256), BF16),
            pltpu.VMEM((D, 256), BF16),
            pltpu.VMEM((256, D), BF16),
            pltpu.VMEM((ROWS, 2 * GROUP, KEY), BF16),
            pltpu.VMEM((CHUNKS, 2, TILES, 16, 128), BF16),
            pltpu.VMEM((CHUNKS, TILES, 16, 128), BF16),
            pltpu.VMEM((ROWS * GROUP, LAT), F32),
            pltpu.VMEM((ROWS * GROUP, 128), F32),
            pltpu.VMEM((EARLY + 1, 16, 128), BF16),
            pltpu.VMEM((CTX, EARLY + 1, 16, 128), BF16),
            pltpu.VMEM((LATE + 1, 16, 128), BF16),
            pltpu.VMEM((CTX, LATE + 1, 16, 128), BF16),
            pltpu.VMEM((ROWS * GROUP, NOPE), F32),
            pltpu.VMEM((2, 16, 128), BF16),
            pltpu.VMEM((HEAD, 2, 16, 128), BF16),
            pltpu.VMEM((2, 16, 128), BF16),
            pltpu.VMEM((CTX, 2, 16, 128), BF16),
            pltpu.VMEM((CTX, 2, 16, 128), BF16),
            pltpu.VMEM((CTX, 2, 16, 128), BF16),
            pltpu.VMEM((HEAD, ROWS, 128), F32),
            pltpu.VMEM((HEAD, ROWS, 128), F32),
            dma((ROWS,)),
            dma((11,)),
            dma((2,)),
            dma((CHUNKS,)),
            dma((CHUNKS,)),
            dma((CTX,)),
            dma((CTX,)),
            dma((CTX,)),
            dma((CTX,)),
            dma((HEAD,)),
            dma((HEAD,)),
            dma((CTX,)),
            dma((CTX,)),
            dma((CTX,)),
            dma((CTX,)),
            dma((HEAD,)),
            dma((HEAD,)),
        ],
        compiler_params=pltpu.CompilerParams(
            collective_id=0, has_side_effects=True, vmem_limit_bytes=60 * 2**20
        ),
    )(
        lengths,
        q_nope,
        q_rope,
        expert_ids,
        gate_weights,
        jnp.swapaxes(latent_cache, 1, 2),
        w_key_absorb,
        w_value_up,
        w_output.T,
        w_gate,
        w_up,
        w_down,
    )
    return pl.pallas_call(
        finish,
        out_shape=(
            jax.ShapeDtypeStruct((ROWS, COLS), BF16),
            jax.ShapeDtypeStruct((ROWS, OUT), BF16),
        ),
        compiler_params=pltpu.CompilerParams(vmem_limit_bytes=2**20),
    )(both)


def solution(mesh):
    return jax.shard_map(
        body,
        mesh=mesh,
        in_specs=(
            P(None, "head", None),
            P(None, "head", None),
            P(None, "ctx", None),
            P(),
            P("head", None, None),
            P("head", None, None),
            P("head", "ctx"),
            P("ctx", None, "head"),
            P("ctx", None, "head"),
            P("ctx", "head", None),
            P(),
            P(),
        ),
        out_specs=(P(None, "ctx"), P(None, ("ctx", "head"))),
        check_vma=False,
    )
```

```python
import functools
import math

import jax
import jax.numpy as jnp
from jax import lax
from jax.experimental import pallas as pl
from jax.experimental.pallas import tpu as pltpu
from jax.sharding import PartitionSpec as P

ROWS = 8
HEADS = 128
NOPE = 128
ROPE = 64
LAT = 512
KEY = LAT + ROPE
D = 7168
CTX = 16
HEAD = 8
GROUP = HEADS // HEAD
SLICE = 8192
SHARERS = (2, 4, 4, 2)
FIRST = (0, 0, 2, 2)
COLS = D // CTX
OUT = COLS // HEAD
CHUNK = 2
CHUNKS = ROWS // CHUNK
TILES = CHUNK * 4 + 1
SCALE = (NOPE + ROPE) ** -0.5 * math.log2(math.e)
EARLY = 4
LATE = ROWS - EARLY
MESH = pl.DeviceIdType.MESH
F32 = jnp.float32
BF16 = jnp.bfloat16


def remote(src, dst, send_sem, recv_sem, device):
    return pltpu.make_async_remote_copy(
        src_ref=src,
        dst_ref=dst,
        send_sem=send_sem,
        recv_sem=recv_sem,
        device_id=device,
        device_id_type=MESH,
    )


def hops(step):
    return sum(min(part, 4 - part) for part in step)


NEAREST = sorted(((dy, dx) for dy in range(4) for dx in range(4) if dy or dx), key=hops)
FARTHEST = NEAREST[::-1]


def loop(low, high, step):
    def run(index, carry):
        step(index)
        return carry

    lax.fori_loop(low, high, run, 0)


def pack(wide):
    wide = wide.astype(BF16).astype(F32)
    first = jnp.concatenate([wide[:, 0:128], wide[:, 128:256]], axis=0).astype(BF16)
    second = jnp.concatenate([wide[:, 256:384], wide[:, 384:512]], axis=0).astype(BF16)
    return first, second


def unpack(first, second):
    first = first.astype(F32)
    second = second.astype(F32)
    return jnp.concatenate([first[0:8], first[8:16], second[0:8], second[8:16]], axis=1)


def split_three(value):
    high = value.astype(BF16).astype(F32)
    rest = value - high
    middle = rest.astype(BF16).astype(F32)
    return high, middle, rest - middle


def lanes(shape):
    return lax.broadcasted_iota(jnp.int32, shape, len(shape) - 1)


def put_levels(levels, rows):
    lane = lanes((rows, 128))
    tile = jnp.zeros((rows, 128), F32)
    for index, level in enumerate(levels):
        for part, value in enumerate(split_three(level)):
            tile = jnp.where(lane == 3 * index + part, value, tile)
    return tile


def get_level(tile, index):
    lane = lanes(tile.shape)
    wanted = (lane >= 3 * index) & (lane < 3 * index + 3)
    return jnp.sum(jnp.where(wanted, tile, 0.0), axis=1, keepdims=True)


def weights_of(levels):
    peak = functools.reduce(jnp.maximum, levels)
    parts = [jnp.exp2(level - peak) for level in levels]
    total = functools.reduce(jnp.add, parts)
    scale = 1.0 / total
    return [part * scale for part in parts], peak + jnp.log2(total)


def kernel(
    lengths_hbm,
    q_nope_hbm,
    q_rope_hbm,
    ids_hbm,
    gates_hbm,
    cache_hbm,
    absorb_hbm,
    value_hbm,
    output_hbm,
    gate_hbm,
    up_hbm,
    down_hbm,
    out_ref,
    lengths_ref,
    q_nope_ref,
    q_rope_ref,
    ids_ref,
    gates_ref,
    keys2,
    keys4,
    values_a,
    values_b,
    absorb,
    value_up,
    w_out,
    w_gate,
    w_up,
    w_down,
    query2,
    query4,
    s1_2,
    r1_2,
    s1_4,
    r1_4,
    whole,
    whole_level,
    s3,
    r3,
    s4,
    r4,
    heads,
    s5,
    r5,
    s6,
    r6,
    s7,
    r7,
    s8,
    r8,
    key_sem,
    weight_sem,
    query2_sem,
    query4_send,
    query4_recv,
    s1_2_sem,
    r1_2_sem,
    s1_4_sem,
    r1_4_sem,
    s3_sem,
    r3_sem,
    s4_sem,
    r4_sem,
    s5_sem,
    r5_sem,
    s6_sem,
    r6_sem,
    s7_sem,
    r7_sem,
    s8_sem,
    r8_sem,
):
    ctx = lax.axis_index("ctx")
    head = lax.axis_index("head")
    keys = {2: keys2, 4: keys4}
    query = {2: query2, 4: query4}
    shares = {
        2: (s1_2, r1_2, s1_2_sem, r1_2_sem),
        4: (s1_4, r1_4, s1_4_sem, r1_4_sem),
    }
    place = {sharers: lax.rem(head, sharers) for sharers in (2, 4)}

    def partner(sharers, step):
        member = lax.rem(place[sharers] + step, sharers)
        return member, {"head": head - place[sharers] + member}

    def other_ctx(step):
        dy, dx = step
        return lax.rem(ctx // 4 + dy, 4) * 4 + lax.rem(lax.rem(ctx, 4) + dx, 4)

    def other_head(step):
        return lax.rem(head + step, HEAD)

    def slot(row):
        chunk = row // CHUNK
        return keys[SHARERS[chunk]].at[FIRST[chunk] + row % CHUNK]

    def key_copy(row):
        sharers = SHARERS[row // CHUNK]
        span = SLICE // sharers
        positions = pl.ds(pl.multiple_of(place[sharers] * span, span), span)
        return pltpu.make_async_copy(
            cache_hbm.at[row, :, positions], slot(row), key_sem.at[row]
        )

    absorb_copy = pltpu.make_async_copy(absorb_hbm, absorb, weight_sem.at[0])
    value_copy = pltpu.make_async_copy(value_hbm, value_up, weight_sem.at[1])
    output_copy = pltpu.make_async_copy(output_hbm, w_out.at[pl.ds(0, COLS)], weight_sem.at[2])
    gate_copy = pltpu.make_async_copy(gate_hbm.at[0], w_gate, weight_sem.at[3])
    up_copy = pltpu.make_async_copy(up_hbm.at[0], w_up, weight_sem.at[4])
    down_copy = pltpu.make_async_copy(down_hbm.at[0], w_down, weight_sem.at[5])
    small_copies = [
        pltpu.make_async_copy(src, dst, weight_sem.at[6 + index])
        for index, (src, dst) in enumerate(
            (
                (q_nope_hbm, q_nope_ref),
                (q_rope_hbm, q_rope_ref),
                (lengths_hbm, lengths_ref),
                (ids_hbm, ids_ref),
                (gates_hbm, gates_ref),
            )
        )
    ]
    small_copies[0].start()
    absorb_copy.start()
    for copy in small_copies[1:]:
        copy.start()
    for row in range(2):
        key_copy(row).start()
    barrier = pltpu.get_barrier_semaphore()

    def greet(device):
        pl.semaphore_signal(barrier, inc=1, device_id=device, device_id_type=MESH)

    for step in FARTHEST:
        greet({"ctx": other_ctx(step)})
    loop(1, HEAD, lambda step: greet({"head": other_head(step)}))
    for row in range(2, 6):
        key_copy(row).start()
    value_copy.start()
    output_copy.start()
    for row in range(6, ROWS):
        key_copy(row).start()
    gate_copy.start()
    up_copy.start()
    down_copy.start()

    w_out[pl.ds(COLS, 512 - COLS), :] = jnp.zeros((512 - COLS, GROUP * NOPE), BF16)
    small_copies[0].wait()
    flat = q_nope_ref[...].reshape(ROWS * GROUP, NOPE).astype(F32)
    which = lax.rem(lax.broadcasted_iota(jnp.int32, (ROWS * GROUP, NOPE), 0), GROUP)
    blocks = [jnp.where(which == h, flat, 0.0).astype(BF16) for h in range(GROUP)]
    wide_query = jnp.concatenate(blocks, axis=1)
    absorb_copy.wait()
    latent = jnp.dot(
        wide_query,
        absorb[...].reshape(GROUP * NOPE, LAT),
        preferred_element_type=F32,
    ).astype(BF16)
    latent = latent.reshape(ROWS, GROUP, LAT)
    small_copies[1].wait()

    def mine(sharers):
        return pl.ds(pl.multiple_of(place[sharers] * GROUP, GROUP), GROUP)

    for chunk in range(CHUNKS):
        held = query[SHARERS[chunk]]
        here = pl.ds(FIRST[chunk], CHUNK)
        rows = slice(chunk * CHUNK, (chunk + 1) * CHUNK)
        held[here, mine(SHARERS[chunk]), 0:LAT] = latent[rows]
        held[here, mine(SHARERS[chunk]), LAT:KEY] = q_rope_ref[rows]
    pl.semaphore_wait(barrier, HEAD - 1 + CTX - 1)
    block2 = query2.at[:, mine(2)]
    query2_copy = remote(
        block2, block2, query2_sem.at[0], query2_sem.at[1], partner(2, 1)[1]
    )
    query2_copy.start()

    def query4_copy(chunk, step, arrival=False):
        member, device = partner(4, step)
        owner = member if arrival else place[4]
        rows = pl.ds(FIRST[chunk], CHUNK)
        block = query4.at[rows, pl.ds(pl.multiple_of(owner * GROUP, GROUP), GROUP)]
        return remote(
            block,
            block,
            query4_send.at[FIRST[chunk] // CHUNK, member],
            query4_recv.at[FIRST[chunk] // CHUNK, owner],
            device,
        )

    for chunk in (1, 2):
        for step in (1, 2, 3):
            query4_copy(chunk, step).start()
    for copy in small_copies[2:]:
        copy.wait()

    def scores(row):
        chunk = row // CHUNK
        sharers = SHARERS[chunk]
        span = SLICE // sharers
        position = ctx * SLICE + place[sharers] * span + lanes((1, span))
        heads_of_row = query[sharers][FIRST[chunk] + row % CHUNK]
        score = jnp.dot(heads_of_row, slot(row)[...], preferred_element_type=F32)
        return jnp.where(position < lengths_ref[row], score, -1e30)

    def soften(score):
        peak = jnp.max(score, axis=1, keepdims=True)
        weight = jnp.exp2((score - peak) * SCALE)
        total = jnp.sum(weight, axis=1, keepdims=True)
        return weight.astype(BF16), 1.0 / total, peak * SCALE + jnp.log2(total)

    def turn(row, values):
        values[0 : SLICE // SHARERS[row // CHUNK], :] = slot(row)[0:LAT, :].T

    def average(weight, values, inverse):
        held = values[0 : weight.shape[1], :]
        return jnp.dot(weight, held, preferred_element_type=F32) * inverse

    key_copy(0).wait()
    turn(0, values_a)
    query2_copy.wait_recv()

    def attend_pair(chunk):
        first = chunk * CHUNK
        more = chunk + 1 < CHUNKS
        key_copy(first + 1).wait()
        score = scores(first)
        turn(first + 1, values_b)
        weight, inverse, level_a = soften(score)
        score = scores(first + 1)
        if more:
            key_copy(first + 2).wait()
        summed_a = average(weight, values_a, inverse)
        if more:
            turn(first + 2, values_a)
        weight, inverse, level_b = soften(score)
        summed_b = average(weight, values_b, inverse)
        return (summed_a, level_a), (summed_b, level_b)

    def share_copy(chunk, step, arrival=False):
        sharers = SHARERS[chunk]
        src, dst, send_sem, recv_sem = shares[sharers]
        member, device = partner(sharers, step)
        source = member if arrival else place[sharers]
        index = FIRST[chunk] // CHUNK
        return remote(
            src.at[index, member],
            dst.at[index, source],
            send_sem.at[index, member],
            recv_sem.at[index, source],
            device,
        )

    def attend(chunk):
        sharers = SHARERS[chunk]
        if sharers == 4:
            for step in (1, 2, 3):
                query4_copy(chunk, step, True).wait_recv()
        results = attend_pair(chunk)
        src = shares[sharers][0]
        index = FIRST[chunk] // CHUNK
        level = put_levels([result[1] for result in results], sharers * GROUP)
        for group in range(sharers):
            rows = slice(group * GROUP, (group + 1) * GROUP)
            for row in range(CHUNK):
                for tile in range(4):
                    src[index, group, row * 4 + tile] = results[row][0][
                        rows, tile * 128 : (tile + 1) * 128
                    ].astype(BF16)
            src[index, group, CHUNK * 4] = level[rows].astype(BF16)
        for step in range(sharers - 1, 0, -1):
            share_copy(chunk, step).start()

    def merge_shares(chunk):
        sharers = SHARERS[chunk]
        src, dst = shares[sharers][0:2]
        index = FIRST[chunk] // CHUNK
        blocks = [src.at[index, place[sharers]]]
        for step in range(1, sharers):
            share_copy(chunk, step, True).wait_recv()
            blocks.append(dst.at[index, partner(sharers, step)[0]])
        tiles = [block[CHUNK * 4].astype(F32) for block in blocks]
        for row in range(CHUNK):
            parts, level = weights_of([get_level(tile, row) for tile in tiles])
            rows = pl.ds((chunk * CHUNK + row) * GROUP, GROUP)
            for tile in range(4):
                whole[rows, tile * 128 : (tile + 1) * 128] = functools.reduce(
                    jnp.add,
                    [
                        block[row * 4 + tile].astype(F32) * part
                        for block, part in zip(blocks, parts)
                    ],
                )
            whole_level[rows, :] = jnp.broadcast_to(level, (GROUP, 128))

    def to_ctx(src, dst, send_sem, recv_sem, step):
        peer = other_ctx(step)
        return remote(src(peer), dst.at[ctx], send_sem.at[peer], recv_sem.at[ctx], {"ctx": peer})

    def from_ctx(src, dst, send_sem, recv_sem, step):
        peer = other_ctx(step)
        return remote(src(peer), dst.at[peer], send_sem.at[peer], recv_sem.at[peer], {"ctx": peer})

    def to_head(src, dst, send_sem, recv_sem, step):
        peer = other_head(step)
        return remote(src(peer), dst.at[head], send_sem.at[peer], recv_sem.at[head], {"head": peer})

    def from_head(src, dst, send_sem, recv_sem, step):
        peer = other_head(step)
        return remote(src(peer), dst.at[peer], send_sem.at[peer], recv_sem.at[peer], {"head": peer})

    exchange3 = (lambda peer: s3, r3, s3_sem, r3_sem)
    exchange4 = (lambda peer: s4, r4, s4_sem, r4_sem)
    exchange5 = (lambda peer: s5, r5, s5_sem, r5_sem)
    exchange6 = (lambda peer: s6, r6, s6_sem, r6_sem)
    exchange7 = (lambda peer: s7.at[peer], r7, s7_sem, r7_sem)
    exchange8 = (lambda peer: s8.at[peer], r8, s8_sem, r8_sem)

    def send_ctx(exchange):
        for step in FARTHEST:
            to_ctx(*exchange, step).start()

    def receive_ctx(exchange):
        for step in NEAREST:
            from_ctx(*exchange, step).wait_recv()

    def project(first, count, exchange):
        rows = pl.ds(first * GROUP, count * GROUP)
        merged = whole[rows, :]
        which = lax.rem(lax.broadcasted_iota(jnp.int32, (count * GROUP, LAT), 0), GROUP)
        blocks = [jnp.where(which == h, merged, 0.0).astype(BF16) for h in range(GROUP)]
        share = jnp.dot(
            jnp.concatenate(blocks, axis=1),
            value_up[...].reshape(GROUP * LAT, NOPE),
            preferred_element_type=F32,
        ).astype(BF16)
        src = exchange[0](0)
        src[0:count] = share.reshape(count, GROUP, NOPE)
        levels = [whole_level[pl.ds((first + row) * GROUP, GROUP), :] for row in range(count)]
        src[count] = put_levels(levels, GROUP).astype(BF16)
        send_ctx(exchange)
        exchange[1][ctx] = src[...]

    def merge_ctx(first, count, exchange):
        receive_ctx(exchange)
        arrived = exchange[1]
        tiles = [arrived[peer, count].astype(F32) for peer in range(CTX)]
        for row in range(count):
            parts, _ = weights_of([get_level(tile, row) for tile in tiles])
            heads[pl.ds((first + row) * GROUP, GROUP), :] = functools.reduce(
                jnp.add, [arrived[peer, row].astype(F32) * parts[peer] for peer in range(CTX)]
            )

    attend(0)
    attend(1)
    merge_shares(0)
    attend(2)
    merge_shares(1)
    value_copy.wait()
    project(0, EARLY, exchange3)
    attend(3)
    merge_shares(2)
    merge_shares(3)
    project(EARLY, LATE, exchange4)
    output_copy.wait()
    values_a[0 : GROUP * NOPE, :] = w_out[...].T
    merge_ctx(0, EARLY, exchange3)
    merge_ctx(EARLY, LATE, exchange4)
    gathered = [heads[pl.ds(member, ROWS, stride=GROUP), :] for member in range(GROUP)]
    partial = jnp.dot(
        jnp.concatenate(gathered, axis=1).astype(BF16),
        values_a[0 : GROUP * NOPE, :],
        preferred_element_type=F32,
    )
    s5[0], s5[1] = pack(partial)
    loop(1, HEAD, lambda step: to_head(*exchange5, step).start())
    r5[head] = s5[...]
    query2_copy.wait_send()
    for chunk in range(CHUNKS):
        for step in range(1, SHARERS[chunk]):
            if SHARERS[chunk] == 4:
                query4_copy(chunk, step).wait_send()
            share_copy(chunk, step).wait_send()
    for exchange in (exchange3, exchange4):
        for step in NEAREST:
            to_ctx(*exchange, step).wait_send()
    loop(1, HEAD, lambda step: from_head(*exchange5, step).wait_recv())
    attn = functools.reduce(jnp.add, [unpack(r5[peer, 0], r5[peer, 1]) for peer in range(HEAD)])
    s6[0], s6[1] = pack(attn)
    send_ctx(exchange6)
    r6[ctx] = s6[...]
    out_ref[:, 0:512] = attn
    gate_copy.wait()
    up_copy.wait()
    squares = jnp.zeros((ROWS, 512), F32)
    gate = jnp.zeros((ROWS, 256), F32)
    upper = jnp.zeros((ROWS, 256), F32)
    for step in [(0, 0)] + NEAREST:
        peer = other_ctx(step)
        if step != (0, 0):
            from_ctx(*exchange6, step).wait_recv()
        features = unpack(r6[peer, 0], r6[peer, 1])
        squares += features * features
        features = features[:, 0:COLS].astype(BF16)
        rows = pl.ds(pl.multiple_of(peer * COLS, COLS), COLS)
        gate += jnp.dot(features, w_gate[rows, :], preferred_element_type=F32)
        upper += jnp.dot(features, w_up[rows, :], preferred_element_type=F32)
    mean = jnp.sum(squares, axis=1, keepdims=True) * (1.0 / D)
    factor = 1.0 / jnp.sqrt(mean + 1e-06)
    gate = gate * factor
    upper = upper * factor
    hidden = (gate / (1.0 + jnp.exp(-gate)) * upper).astype(BF16)
    chosen = jnp.where(ids_ref[...] == ctx, gates_ref[...], 0.0)
    select = jnp.sum(chosen, axis=1, keepdims=True)
    down_copy.wait()
    result = jnp.dot(hidden, w_down[...], preferred_element_type=F32) * select
    for peer in range(CTX):
        left = peer * COLS // 128 * 128
        s7[peer, 0], s7[peer, 1] = pack(result[:, left : left + 512])
    send_ctx(exchange7)
    share = unpack(s7[ctx, 0], s7[ctx, 1])
    for step in NEAREST:
        peer = other_ctx(step)
        from_ctx(*exchange7, step).wait_recv()
        share += unpack(r7[peer, 0], r7[peer, 1])
    share = jnp.where(lax.rem(ctx, 2) == 1, pltpu.roll(share, 512 - COLS % 128, 1), share)
    for peer in range(HEAD):
        moved = share if peer == 0 else pltpu.roll(share, 512 - peer * OUT, 1)
        s8[peer] = moved[:, 0:128]
    loop(1, HEAD, lambda step: to_head(*exchange8, step).start())
    r8[head] = s8[head]
    for step in NEAREST:
        to_ctx(*exchange6, step).wait_send()
    loop(1, HEAD, lambda step: to_head(*exchange5, step).wait_send())
    loop(1, HEAD, lambda step: from_head(*exchange8, step).wait_recv())
    out_ref[:, 512:640] = functools.reduce(jnp.add, [r8[peer] for peer in range(HEAD)])

    for step in NEAREST:
        to_ctx(*exchange7, step).wait_send()
    loop(1, HEAD, lambda step: to_head(*exchange8, step).wait_send())


def finish(both_ref, attn_ref, expert_ref):
    attn_ref[...] = both_ref[:, 0:COLS].astype(BF16)
    expert_ref[...] = both_ref[:, 512 : 512 + OUT].astype(BF16)


def body(
    q_nope,
    q_rope,
    latent_cache,
    lengths,
    w_key_absorb,
    w_value_up,
    w_output,
    w_gate,
    w_up,
    w_down,
    expert_ids,
    gate_weights,
):
    vmem = pl.BlockSpec(memory_space=pltpu.VMEM)
    hbm = pl.BlockSpec(memory_space=pl.ANY)
    dma = pltpu.SemaphoreType.DMA
    both = pl.pallas_call(
        kernel,
        out_shape=pltpu.VMEM((ROWS, 640), F32),
        in_specs=[hbm] * 12,
        out_specs=vmem,
        scratch_shapes=[
            pltpu.SMEM((ROWS,), jnp.int32),
            pltpu.VMEM((ROWS, GROUP, NOPE), BF16),
            pltpu.VMEM((ROWS, GROUP, ROPE), BF16),
            pltpu.VMEM((ROWS, 8), jnp.int32),
            pltpu.VMEM((ROWS, 8), F32),
            pltpu.VMEM((4, KEY, SLICE // 2), BF16),
            pltpu.VMEM((4, KEY, SLICE // 4), BF16),
            pltpu.VMEM((SLICE // 2, LAT), BF16),
            pltpu.VMEM((SLICE // 2, LAT), BF16),
            pltpu.VMEM((GROUP, NOPE, LAT), BF16),
            pltpu.VMEM((GROUP, LAT, NOPE), BF16),
            pltpu.VMEM((512, GROUP * NOPE), BF16),
            pltpu.VMEM((D, 256), BF16),
            pltpu.VMEM((D, 256), BF16),
            pltpu.VMEM((256, D), BF16),
            pltpu.VMEM((4, 2 * GROUP, KEY), BF16),
            pltpu.VMEM((4, 4 * GROUP, KEY), BF16),
            pltpu.VMEM((2, 2, TILES, 16, 128), BF16),
            pltpu.VMEM((2, 2, TILES, 16, 128), BF16),
            pltpu.VMEM((2, 4, TILES, 16, 128), BF16),
            pltpu.VMEM((2, 4, TILES, 16, 128), BF16),
            pltpu.VMEM((ROWS * GROUP, LAT), F32),
            pltpu.VMEM((ROWS * GROUP, 128), F32),
            pltpu.VMEM((EARLY + 1, 16, 128), BF16),
            pltpu.VMEM((CTX, EARLY + 1, 16, 128), BF16),
            pltpu.VMEM((LATE + 1, 16, 128), BF16),
            pltpu.VMEM((CTX, LATE + 1, 16, 128), BF16),
            pltpu.VMEM((ROWS * GROUP, NOPE), F32),
            pltpu.VMEM((2, 16, 128), BF16),
            pltpu.VMEM((HEAD, 2, 16, 128), BF16),
            pltpu.VMEM((2, 16, 128), BF16),
            pltpu.VMEM((CTX, 2, 16, 128), BF16),
            pltpu.VMEM((CTX, 2, 16, 128), BF16),
            pltpu.VMEM((CTX, 2, 16, 128), BF16),
            pltpu.VMEM((HEAD, ROWS, 128), F32),
            pltpu.VMEM((HEAD, ROWS, 128), F32),
            dma((ROWS,)),
            dma((11,)),
            dma((2,)),
            dma((2, 4)),
            dma((2, 4)),
            dma((2, 2)),
            dma((2, 2)),
            dma((2, 4)),
            dma((2, 4)),
            dma((CTX,)),
            dma((CTX,)),
            dma((CTX,)),
            dma((CTX,)),
            dma((HEAD,)),
            dma((HEAD,)),
            dma((CTX,)),
            dma((CTX,)),
            dma((CTX,)),
            dma((CTX,)),
            dma((HEAD,)),
            dma((HEAD,)),
        ],
        compiler_params=pltpu.CompilerParams(
            collective_id=0, has_side_effects=True, vmem_limit_bytes=60 * 2**20
        ),
    )(
        lengths,
        q_nope,
        q_rope,
        expert_ids,
        gate_weights,
        jnp.swapaxes(latent_cache, 1, 2),
        w_key_absorb,
        w_value_up,
        w_output.T,
        w_gate,
        w_up,
        w_down,
    )
    return pl.pallas_call(
        finish,
        out_shape=(
            jax.ShapeDtypeStruct((ROWS, COLS), BF16),
            jax.ShapeDtypeStruct((ROWS, OUT), BF16),
        ),
        compiler_params=pltpu.CompilerParams(vmem_limit_bytes=2**20),
    )(both)


def solution(mesh):
    return jax.shard_map(
        body,
        mesh=mesh,
        in_specs=(
            P(None, "head", None),
            P(None, "head", None),
            P(None, "ctx", None),
            P(),
            P("head", None, None),
            P("head", None, None),
            P("head", "ctx"),
            P("ctx", None, "head"),
            P("ctx", None, "head"),
            P("ctx", "head", None),
            P(),
            P(),
        ),
        out_specs=(P(None, "ctx"), P(None, ("ctx", "head"))),
        check_vma=False,
    )
```

```python
import functools
import math

import jax
import jax.numpy as jnp
from jax import lax
from jax.experimental import pallas as pl
from jax.experimental.pallas import tpu as pltpu
from jax.sharding import PartitionSpec as P

ROWS = 8
HEADS = 128
NOPE = 128
ROPE = 64
LAT = 512
KEY = LAT + ROPE
D = 7168
CTX = 16
HEAD = 8
GROUP = HEADS // HEAD
SLICE = 8192
SHARERS = (2, 4, 4, 2)
FIRST = (0, 0, 2, 2)
COLS = D // CTX
OUT = COLS // HEAD
CHUNK = 2
CHUNKS = ROWS // CHUNK
TILES = CHUNK * 4 + 1
SCALE = (NOPE + ROPE) ** -0.5 * math.log2(math.e)
EARLY = 4
LATE = ROWS - EARLY
MESH = pl.DeviceIdType.MESH
F32 = jnp.float32
BF16 = jnp.bfloat16


def remote(src, dst, send_sem, recv_sem, device):
    return pltpu.make_async_remote_copy(
        src_ref=src,
        dst_ref=dst,
        send_sem=send_sem,
        recv_sem=recv_sem,
        device_id=device,
        device_id_type=MESH,
    )


def hops(step):
    return sum(min(part, 4 - part) for part in step)


NEAREST = sorted(((dy, dx) for dy in range(4) for dx in range(4) if dy or dx), key=hops)
FARTHEST = NEAREST[::-1]


def loop(low, high, step):
    def run(index, carry):
        step(index)
        return carry

    lax.fori_loop(low, high, run, 0)


def pack(wide):
    wide = wide.astype(BF16).astype(F32)
    first = jnp.concatenate([wide[:, 0:128], wide[:, 128:256]], axis=0).astype(BF16)
    second = jnp.concatenate([wide[:, 256:384], wide[:, 384:512]], axis=0).astype(BF16)
    return first, second


def unpack(first, second):
    first = first.astype(F32)
    second = second.astype(F32)
    return jnp.concatenate([first[0:8], first[8:16], second[0:8], second[8:16]], axis=1)


def split_three(value):
    high = value.astype(BF16).astype(F32)
    rest = value - high
    middle = rest.astype(BF16).astype(F32)
    return high, middle, rest - middle


def lanes(shape):
    return lax.broadcasted_iota(jnp.int32, shape, len(shape) - 1)


def put_levels(levels, rows):
    lane = lanes((rows, 128))
    tile = jnp.zeros((rows, 128), F32)
    for index, level in enumerate(levels):
        for part, value in enumerate(split_three(level)):
            tile = jnp.where(lane == 3 * index + part, value, tile)
    return tile


def get_level(tile, index):
    lane = lanes(tile.shape)
    wanted = (lane >= 3 * index) & (lane < 3 * index + 3)
    return jnp.sum(jnp.where(wanted, tile, 0.0), axis=1, keepdims=True)


def weights_of(levels):
    peak = functools.reduce(jnp.maximum, levels)
    parts = [jnp.exp2(level - peak) for level in levels]
    total = functools.reduce(jnp.add, parts)
    scale = 1.0 / total
    return [part * scale for part in parts], peak + jnp.log2(total)


def kernel(
    lengths_hbm,
    q_nope_hbm,
    q_rope_hbm,
    ids_hbm,
    gates_hbm,
    cache_hbm,
    absorb_hbm,
    value_hbm,
    output_hbm,
    gate_hbm,
    up_hbm,
    down_hbm,
    out_ref,
    lengths_ref,
    q_nope_ref,
    q_rope_ref,
    ids_ref,
    gates_ref,
    keys2,
    keys4,
    values_a,
    values_b,
    absorb,
    value_up,
    w_out,
    w_gate,
    w_up,
    w_down,
    query2,
    query4,
    s1_2,
    r1_2,
    s1_4,
    r1_4,
    whole,
    whole_level,
    s3,
    r3,
    s4,
    r4,
    heads,
    s5,
    r5,
    s6,
    r6,
    s7,
    r7,
    s8,
    r8,
    key_sem,
    weight_sem,
    query2_sem,
    query4_send,
    query4_recv,
    s1_2_sem,
    r1_2_sem,
    s1_4_sem,
    r1_4_sem,
    s3_sem,
    r3_sem,
    s4_sem,
    r4_sem,
    s5_sem,
    r5_sem,
    s6_sem,
    r6_sem,
    s7_sem,
    r7_sem,
    s8_sem,
    r8_sem,
):
    ctx = lax.axis_index("ctx")
    head = lax.axis_index("head")
    keys = {2: keys2, 4: keys4}
    query = {2: query2, 4: query4}
    shares = {
        2: (s1_2, r1_2, s1_2_sem, r1_2_sem),
        4: (s1_4, r1_4, s1_4_sem, r1_4_sem),
    }
    place = {sharers: lax.rem(head, sharers) for sharers in (2, 4)}

    def partner(sharers, step):
        member = lax.rem(place[sharers] + step, sharers)
        return member, {"head": head - place[sharers] + member}

    def other_ctx(step):
        dy, dx = step
        return lax.rem(ctx // 4 + dy, 4) * 4 + lax.rem(lax.rem(ctx, 4) + dx, 4)

    def other_head(step):
        return lax.rem(head + step, HEAD)

    def slot(row):
        chunk = row // CHUNK
        return keys[SHARERS[chunk]].at[FIRST[chunk] + row % CHUNK]

    def key_copy(row):
        sharers = SHARERS[row // CHUNK]
        span = SLICE // sharers
        positions = pl.ds(pl.multiple_of(place[sharers] * span, span), span)
        return pltpu.make_async_copy(
            cache_hbm.at[row, :, positions], slot(row), key_sem.at[row]
        )

    absorb_copy = pltpu.make_async_copy(absorb_hbm, absorb, weight_sem.at[0])
    value_copy = pltpu.make_async_copy(value_hbm, value_up, weight_sem.at[1])
    output_copy = pltpu.make_async_copy(output_hbm, w_out.at[pl.ds(0, COLS)], weight_sem.at[2])
    gate_copy = pltpu.make_async_copy(gate_hbm.at[0], w_gate, weight_sem.at[3])
    up_copy = pltpu.make_async_copy(up_hbm.at[0], w_up, weight_sem.at[4])
    down_copy = pltpu.make_async_copy(down_hbm.at[0], w_down, weight_sem.at[5])
    small_copies = [
        pltpu.make_async_copy(src, dst, weight_sem.at[6 + index])
        for index, (src, dst) in enumerate(
            (
                (q_nope_hbm, q_nope_ref),
                (q_rope_hbm, q_rope_ref),
                (lengths_hbm, lengths_ref),
                (ids_hbm, ids_ref),
                (gates_hbm, gates_ref),
            )
        )
    ]
    small_copies[0].start()
    absorb_copy.start()
    for copy in small_copies[1:]:
        copy.start()
    for row in range(2):
        key_copy(row).start()
    barrier = pltpu.get_barrier_semaphore()

    def greet(device):
        pl.semaphore_signal(barrier, inc=1, device_id=device, device_id_type=MESH)

    for step in FARTHEST:
        greet({"ctx": other_ctx(step)})
    loop(1, HEAD, lambda step: greet({"head": other_head(step)}))
    for row in range(2, 6):
        key_copy(row).start()
    value_copy.start()
    output_copy.start()
    for row in range(6, ROWS):
        key_copy(row).start()
    gate_copy.start()
    up_copy.start()
    down_copy.start()

    w_out[pl.ds(COLS, 512 - COLS), :] = jnp.zeros((512 - COLS, GROUP * NOPE), BF16)
    small_copies[0].wait()
    flat = q_nope_ref[...].reshape(ROWS * GROUP, NOPE).astype(F32)
    which = lax.rem(lax.broadcasted_iota(jnp.int32, (ROWS * GROUP, NOPE), 0), GROUP)
    blocks = [jnp.where(which == h, flat, 0.0).astype(BF16) for h in range(GROUP)]
    wide_query = jnp.concatenate(blocks, axis=1)
    absorb_copy.wait()
    latent = jnp.dot(
        wide_query,
        absorb[...].reshape(GROUP * NOPE, LAT),
        preferred_element_type=F32,
    ).astype(BF16)
    latent = latent.reshape(ROWS, GROUP, LAT)
    small_copies[1].wait()

    def mine(sharers):
        return pl.ds(pl.multiple_of(place[sharers] * GROUP, GROUP), GROUP)

    for chunk in range(CHUNKS):
        held = query[SHARERS[chunk]]
        here = pl.ds(FIRST[chunk], CHUNK)
        rows = slice(chunk * CHUNK, (chunk + 1) * CHUNK)
        held[here, mine(SHARERS[chunk]), 0:LAT] = latent[rows]
        held[here, mine(SHARERS[chunk]), LAT:KEY] = q_rope_ref[rows]
    pl.semaphore_wait(barrier, HEAD - 1 + CTX - 1)
    block2 = query2.at[:, mine(2)]
    query2_copy = remote(
        block2, block2, query2_sem.at[0], query2_sem.at[1], partner(2, 1)[1]
    )
    query2_copy.start()

    def query4_copy(chunk, step, arrival=False):
        member, device = partner(4, step)
        owner = member if arrival else place[4]
        rows = pl.ds(FIRST[chunk], CHUNK)
        block = query4.at[rows, pl.ds(pl.multiple_of(owner * GROUP, GROUP), GROUP)]
        return remote(
            block,
            block,
            query4_send.at[FIRST[chunk] // CHUNK, member],
            query4_recv.at[FIRST[chunk] // CHUNK, owner],
            device,
        )

    for chunk in (1, 2):
        for step in (1, 2, 3):
            query4_copy(chunk, step).start()
    for copy in small_copies[2:]:
        copy.wait()

    def scores(row):
        chunk = row // CHUNK
        sharers = SHARERS[chunk]
        span = SLICE // sharers
        position = ctx * SLICE + place[sharers] * span + lanes((1, span))
        heads_of_row = query[sharers][FIRST[chunk] + row % CHUNK]
        score = jnp.dot(heads_of_row, slot(row)[...], preferred_element_type=F32)
        return jnp.where(position < lengths_ref[row], score, -1e30)

    def soften(score):
        peak = jnp.max(score, axis=1, keepdims=True)
        weight = jnp.exp2((score - peak) * SCALE)
        total = jnp.sum(weight, axis=1, keepdims=True)
        return weight.astype(BF16), 1.0 / total, peak * SCALE + jnp.log2(total)

    def turn(row, values):
        values[0 : SLICE // SHARERS[row // CHUNK], :] = slot(row)[0:LAT, :].T

    def average(weight, values, inverse):
        held = values[0 : weight.shape[1], :]
        return jnp.dot(weight, held, preferred_element_type=F32) * inverse

    key_copy(0).wait()
    turn(0, values_a)
    query2_copy.wait_recv()

    def nothing():
        pass

    def attend_pair(chunk, before, between):
        first = chunk * CHUNK
        more = chunk + 1 < CHUNKS
        key_copy(first + 1).wait()
        before()
        score = scores(first)
        turn(first + 1, values_b)
        weight, inverse, level_a = soften(score)
        score = scores(first + 1)
        if more:
            key_copy(first + 2).wait()
        between()
        summed_a = average(weight, values_a, inverse)
        if more:
            turn(first + 2, values_a)
        weight, inverse, level_b = soften(score)
        summed_b = average(weight, values_b, inverse)
        return (summed_a, level_a), (summed_b, level_b)

    def share_copy(chunk, step, arrival=False):
        sharers = SHARERS[chunk]
        src, dst, send_sem, recv_sem = shares[sharers]
        member, device = partner(sharers, step)
        source = member if arrival else place[sharers]
        index = FIRST[chunk] // CHUNK
        return remote(
            src.at[index, member],
            dst.at[index, source],
            send_sem.at[index, member],
            recv_sem.at[index, source],
            device,
        )

    def attend(chunk, before=nothing, between=nothing):
        sharers = SHARERS[chunk]
        if sharers == 4:
            for step in (1, 2, 3):
                query4_copy(chunk, step, True).wait_recv()
        results = attend_pair(chunk, before, between)
        src = shares[sharers][0]
        index = FIRST[chunk] // CHUNK
        level = put_levels([result[1] for result in results], sharers * GROUP)
        for group in range(sharers):
            rows = slice(group * GROUP, (group + 1) * GROUP)
            for row in range(CHUNK):
                for tile in range(4):
                    src[index, group, row * 4 + tile] = results[row][0][
                        rows, tile * 128 : (tile + 1) * 128
                    ].astype(BF16)
            src[index, group, CHUNK * 4] = level[rows].astype(BF16)
        for step in range(sharers - 1, 0, -1):
            share_copy(chunk, step).start()

    def receive_shares(chunk):
        for step in range(1, SHARERS[chunk]):
            share_copy(chunk, step, True).wait_recv()

    def merge_shares(chunk):
        sharers = SHARERS[chunk]
        src, dst = shares[sharers][0:2]
        index = FIRST[chunk] // CHUNK
        blocks = [src.at[index, place[sharers]]]
        for step in range(1, sharers):
            blocks.append(dst.at[index, partner(sharers, step)[0]])
        tiles = [block[CHUNK * 4].astype(F32) for block in blocks]
        for row in range(CHUNK):
            parts, level = weights_of([get_level(tile, row) for tile in tiles])
            rows = pl.ds((chunk * CHUNK + row) * GROUP, GROUP)
            for tile in range(4):
                whole[rows, tile * 128 : (tile + 1) * 128] = functools.reduce(
                    jnp.add,
                    [
                        block[row * 4 + tile].astype(F32) * part
                        for block, part in zip(blocks, parts)
                    ],
                )
            whole_level[rows, :] = jnp.broadcast_to(level, (GROUP, 128))

    def to_ctx(src, dst, send_sem, recv_sem, step):
        peer = other_ctx(step)
        return remote(src(peer), dst.at[ctx], send_sem.at[peer], recv_sem.at[ctx], {"ctx": peer})

    def from_ctx(src, dst, send_sem, recv_sem, step):
        peer = other_ctx(step)
        return remote(src(peer), dst.at[peer], send_sem.at[peer], recv_sem.at[peer], {"ctx": peer})

    def to_head(src, dst, send_sem, recv_sem, step):
        peer = other_head(step)
        return remote(src(peer), dst.at[head], send_sem.at[peer], recv_sem.at[head], {"head": peer})

    def from_head(src, dst, send_sem, recv_sem, step):
        peer = other_head(step)
        return remote(src(peer), dst.at[peer], send_sem.at[peer], recv_sem.at[peer], {"head": peer})

    exchange3 = (lambda peer: s3, r3, s3_sem, r3_sem)
    exchange4 = (lambda peer: s4, r4, s4_sem, r4_sem)
    exchange5 = (lambda peer: s5, r5, s5_sem, r5_sem)
    exchange6 = (lambda peer: s6, r6, s6_sem, r6_sem)
    exchange7 = (lambda peer: s7.at[peer], r7, s7_sem, r7_sem)
    exchange8 = (lambda peer: s8.at[peer], r8, s8_sem, r8_sem)

    def send_ctx(exchange):
        for step in FARTHEST:
            to_ctx(*exchange, step).start()

    def receive_ctx(exchange):
        for step in NEAREST:
            from_ctx(*exchange, step).wait_recv()

    def project(first, count, exchange):
        rows = pl.ds(first * GROUP, count * GROUP)
        merged = whole[rows, :]
        which = lax.rem(lax.broadcasted_iota(jnp.int32, (count * GROUP, LAT), 0), GROUP)
        blocks = [jnp.where(which == h, merged, 0.0).astype(BF16) for h in range(GROUP)]
        share = jnp.dot(
            jnp.concatenate(blocks, axis=1),
            value_up[...].reshape(GROUP * LAT, NOPE),
            preferred_element_type=F32,
        ).astype(BF16)
        src = exchange[0](0)
        src[0:count] = share.reshape(count, GROUP, NOPE)
        levels = [whole_level[pl.ds((first + row) * GROUP, GROUP), :] for row in range(count)]
        src[count] = put_levels(levels, GROUP).astype(BF16)
        send_ctx(exchange)
        exchange[1][ctx] = src[...]

    def merge_ctx(first, count, exchange):
        receive_ctx(exchange)
        arrived = exchange[1]
        tiles = [arrived[peer, count].astype(F32) for peer in range(CTX)]
        for row in range(count):
            parts, _ = weights_of([get_level(tile, row) for tile in tiles])
            heads[pl.ds((first + row) * GROUP, GROUP), :] = functools.reduce(
                jnp.add, [arrived[peer, row].astype(F32) * parts[peer] for peer in range(CTX)]
            )

    def send_early():
        receive_shares(1)
        value_copy.wait()
        merge_shares(1)
        project(0, EARLY, exchange3)

    attend(0)
    attend(1)
    receive_shares(0)
    attend(2, before=lambda: merge_shares(0))
    attend(3, between=send_early)
    receive_shares(2)
    merge_shares(2)
    receive_shares(3)
    merge_shares(3)
    project(EARLY, LATE, exchange4)
    output_copy.wait()
    values_a[0 : GROUP * NOPE, :] = w_out[...].T
    merge_ctx(0, EARLY, exchange3)
    merge_ctx(EARLY, LATE, exchange4)
    gathered = [heads[pl.ds(member, ROWS, stride=GROUP), :] for member in range(GROUP)]
    partial = jnp.dot(
        jnp.concatenate(gathered, axis=1).astype(BF16),
        values_a[0 : GROUP * NOPE, :],
        preferred_element_type=F32,
    )
    s5[0], s5[1] = pack(partial)
    loop(1, HEAD, lambda step: to_head(*exchange5, step).start())
    r5[head] = s5[...]
    query2_copy.wait_send()
    for chunk in range(CHUNKS):
        for step in range(1, SHARERS[chunk]):
            if SHARERS[chunk] == 4:
                query4_copy(chunk, step).wait_send()
            share_copy(chunk, step).wait_send()
    for exchange in (exchange3, exchange4):
        for step in NEAREST:
            to_ctx(*exchange, step).wait_send()
    loop(1, HEAD, lambda step: from_head(*exchange5, step).wait_recv())
    attn = functools.reduce(jnp.add, [unpack(r5[peer, 0], r5[peer, 1]) for peer in range(HEAD)])
    s6[0], s6[1] = pack(attn)
    send_ctx(exchange6)
    r6[ctx] = s6[...]
    out_ref[:, 0:512] = attn
    gate_copy.wait()
    up_copy.wait()
    squares = jnp.zeros((ROWS, 512), F32)
    gate = jnp.zeros((ROWS, 256), F32)
    upper = jnp.zeros((ROWS, 256), F32)
    for step in [(0, 0)] + NEAREST:
        peer = other_ctx(step)
        if step != (0, 0):
            from_ctx(*exchange6, step).wait_recv()
        features = unpack(r6[peer, 0], r6[peer, 1])
        squares += features * features
        features = features[:, 0:COLS].astype(BF16)
        rows = pl.ds(pl.multiple_of(peer * COLS, COLS), COLS)
        gate += jnp.dot(features, w_gate[rows, :], preferred_element_type=F32)
        upper += jnp.dot(features, w_up[rows, :], preferred_element_type=F32)
    mean = jnp.sum(squares, axis=1, keepdims=True) * (1.0 / D)
    factor = 1.0 / jnp.sqrt(mean + 1e-06)
    gate = gate * factor
    upper = upper * factor
    hidden = (gate / (1.0 + jnp.exp(-gate)) * upper).astype(BF16)
    chosen = jnp.where(ids_ref[...] == ctx, gates_ref[...], 0.0)
    select = jnp.sum(chosen, axis=1, keepdims=True)
    down_copy.wait()
    result = jnp.dot(hidden, w_down[...], preferred_element_type=F32) * select
    for peer in range(CTX):
        left = peer * COLS // 128 * 128
        s7[peer, 0], s7[peer, 1] = pack(result[:, left : left + 512])
    send_ctx(exchange7)
    share = unpack(s7[ctx, 0], s7[ctx, 1])
    for step in NEAREST:
        peer = other_ctx(step)
        from_ctx(*exchange7, step).wait_recv()
        share += unpack(r7[peer, 0], r7[peer, 1])
    share = jnp.where(lax.rem(ctx, 2) == 1, pltpu.roll(share, 512 - COLS % 128, 1), share)
    for peer in range(HEAD):
        moved = share if peer == 0 else pltpu.roll(share, 512 - peer * OUT, 1)
        s8[peer] = moved[:, 0:128]
    loop(1, HEAD, lambda step: to_head(*exchange8, step).start())
    r8[head] = s8[head]
    for step in NEAREST:
        to_ctx(*exchange6, step).wait_send()
    loop(1, HEAD, lambda step: to_head(*exchange5, step).wait_send())
    loop(1, HEAD, lambda step: from_head(*exchange8, step).wait_recv())
    out_ref[:, 512:640] = functools.reduce(jnp.add, [r8[peer] for peer in range(HEAD)])

    for step in NEAREST:
        to_ctx(*exchange7, step).wait_send()
    loop(1, HEAD, lambda step: to_head(*exchange8, step).wait_send())


def finish(both_ref, attn_ref, expert_ref):
    attn_ref[...] = both_ref[:, 0:COLS].astype(BF16)
    expert_ref[...] = both_ref[:, 512 : 512 + OUT].astype(BF16)


def body(
    q_nope,
    q_rope,
    latent_cache,
    lengths,
    w_key_absorb,
    w_value_up,
    w_output,
    w_gate,
    w_up,
    w_down,
    expert_ids,
    gate_weights,
):
    vmem = pl.BlockSpec(memory_space=pltpu.VMEM)
    hbm = pl.BlockSpec(memory_space=pl.ANY)
    dma = pltpu.SemaphoreType.DMA
    both = pl.pallas_call(
        kernel,
        out_shape=pltpu.VMEM((ROWS, 640), F32),
        in_specs=[hbm] * 12,
        out_specs=vmem,
        scratch_shapes=[
            pltpu.SMEM((ROWS,), jnp.int32),
            pltpu.VMEM((ROWS, GROUP, NOPE), BF16),
            pltpu.VMEM((ROWS, GROUP, ROPE), BF16),
            pltpu.VMEM((ROWS, 8), jnp.int32),
            pltpu.VMEM((ROWS, 8), F32),
            pltpu.VMEM((4, KEY, SLICE // 2), BF16),
            pltpu.VMEM((4, KEY, SLICE // 4), BF16),
            pltpu.VMEM((SLICE // 2, LAT), BF16),
            pltpu.VMEM((SLICE // 2, LAT), BF16),
            pltpu.VMEM((GROUP, NOPE, LAT), BF16),
            pltpu.VMEM((GROUP, LAT, NOPE), BF16),
            pltpu.VMEM((512, GROUP * NOPE), BF16),
            pltpu.VMEM((D, 256), BF16),
            pltpu.VMEM((D, 256), BF16),
            pltpu.VMEM((256, D), BF16),
            pltpu.VMEM((4, 2 * GROUP, KEY), BF16),
            pltpu.VMEM((4, 4 * GROUP, KEY), BF16),
            pltpu.VMEM((2, 2, TILES, 16, 128), BF16),
            pltpu.VMEM((2, 2, TILES, 16, 128), BF16),
            pltpu.VMEM((2, 4, TILES, 16, 128), BF16),
            pltpu.VMEM((2, 4, TILES, 16, 128), BF16),
            pltpu.VMEM((ROWS * GROUP, LAT), F32),
            pltpu.VMEM((ROWS * GROUP, 128), F32),
            pltpu.VMEM((EARLY + 1, 16, 128), BF16),
            pltpu.VMEM((CTX, EARLY + 1, 16, 128), BF16),
            pltpu.VMEM((LATE + 1, 16, 128), BF16),
            pltpu.VMEM((CTX, LATE + 1, 16, 128), BF16),
            pltpu.VMEM((ROWS * GROUP, NOPE), F32),
            pltpu.VMEM((2, 16, 128), BF16),
            pltpu.VMEM((HEAD, 2, 16, 128), BF16),
            pltpu.VMEM((2, 16, 128), BF16),
            pltpu.VMEM((CTX, 2, 16, 128), BF16),
            pltpu.VMEM((CTX, 2, 16, 128), BF16),
            pltpu.VMEM((CTX, 2, 16, 128), BF16),
            pltpu.VMEM((HEAD, ROWS, 128), F32),
            pltpu.VMEM((HEAD, ROWS, 128), F32),
            dma((ROWS,)),
            dma((11,)),
            dma((2,)),
            dma((2, 4)),
            dma((2, 4)),
            dma((2, 2)),
            dma((2, 2)),
            dma((2, 4)),
            dma((2, 4)),
            dma((CTX,)),
            dma((CTX,)),
            dma((CTX,)),
            dma((CTX,)),
            dma((HEAD,)),
            dma((HEAD,)),
            dma((CTX,)),
            dma((CTX,)),
            dma((CTX,)),
            dma((CTX,)),
            dma((HEAD,)),
            dma((HEAD,)),
        ],
        compiler_params=pltpu.CompilerParams(
            collective_id=0, has_side_effects=True, vmem_limit_bytes=60 * 2**20
        ),
    )(
        lengths,
        q_nope,
        q_rope,
        expert_ids,
        gate_weights,
        jnp.swapaxes(latent_cache, 1, 2),
        w_key_absorb,
        w_value_up,
        w_output.T,
        w_gate,
        w_up,
        w_down,
    )
    return pl.pallas_call(
        finish,
        out_shape=(
            jax.ShapeDtypeStruct((ROWS, COLS), BF16),
            jax.ShapeDtypeStruct((ROWS, OUT), BF16),
        ),
        compiler_params=pltpu.CompilerParams(vmem_limit_bytes=2**20),
    )(both)


def solution(mesh):
    return jax.shard_map(
        body,
        mesh=mesh,
        in_specs=(
            P(None, "head", None),
            P(None, "head", None),
            P(None, "ctx", None),
            P(),
            P("head", None, None),
            P("head", None, None),
            P("head", "ctx"),
            P("ctx", None, "head"),
            P("ctx", None, "head"),
            P("ctx", "head", None),
            P(),
            P(),
        ),
        out_specs=(P(None, "ctx"), P(None, ("ctx", "head"))),
        check_vma=False,
    )
```

```python
import functools
import math

import jax
import jax.numpy as jnp
from jax import lax
from jax.experimental import pallas as pl
from jax.experimental.pallas import tpu as pltpu
from jax.sharding import PartitionSpec as P

ROWS = 8
HEADS = 128
NOPE = 128
ROPE = 64
LAT = 512
KEY = LAT + ROPE
D = 7168
CTX = 16
HEAD = 8
GROUP = HEADS // HEAD
SLICE = 8192
SHARERS = (2, 4, 4, 2)
FIRST = (0, 0, 2, 2)
COLS = D // CTX
OUT = COLS // HEAD
CHUNK = 2
CHUNKS = ROWS // CHUNK
TILES = CHUNK * 4 + 1
SCALE = (NOPE + ROPE) ** -0.5 * math.log2(math.e)
EARLY = 4
LATE = ROWS - EARLY
MESH = pl.DeviceIdType.MESH
F32 = jnp.float32
BF16 = jnp.bfloat16


def remote(src, dst, send_sem, recv_sem, device):
    return pltpu.make_async_remote_copy(
        src_ref=src,
        dst_ref=dst,
        send_sem=send_sem,
        recv_sem=recv_sem,
        device_id=device,
        device_id_type=MESH,
    )


def hops(step):
    return sum(min(part, 4 - part) for part in step)


NEAREST = sorted(((dy, dx) for dy in range(4) for dx in range(4) if dy or dx), key=hops)
FARTHEST = NEAREST[::-1]
HEAD_STEPS = (4, 5, 3, 2, 6, 1, 7)


def loop(low, high, step):
    def run(index, carry):
        step(index)
        return carry

    lax.fori_loop(low, high, run, 0)


def pack(wide):
    wide = wide.astype(BF16).astype(F32)
    first = jnp.concatenate([wide[:, 0:128], wide[:, 128:256]], axis=0).astype(BF16)
    second = jnp.concatenate([wide[:, 256:384], wide[:, 384:512]], axis=0).astype(BF16)
    return first, second


def unpack(first, second):
    first = first.astype(F32)
    second = second.astype(F32)
    return jnp.concatenate([first[0:8], first[8:16], second[0:8], second[8:16]], axis=1)


def split_three(value):
    high = value.astype(BF16).astype(F32)
    rest = value - high
    middle = rest.astype(BF16).astype(F32)
    return high, middle, rest - middle


def lanes(shape):
    return lax.broadcasted_iota(jnp.int32, shape, len(shape) - 1)


def put_levels(levels, rows):
    lane = lanes((rows, 128))
    tile = jnp.zeros((rows, 128), F32)
    for index, level in enumerate(levels):
        for part, value in enumerate(split_three(level)):
            tile = jnp.where(lane == 3 * index + part, value, tile)
    return tile


def get_level(tile, index):
    lane = lanes(tile.shape)
    wanted = (lane >= 3 * index) & (lane < 3 * index + 3)
    return jnp.sum(jnp.where(wanted, tile, 0.0), axis=1, keepdims=True)


def weights_of(levels):
    peak = functools.reduce(jnp.maximum, levels)
    parts = [jnp.exp2(level - peak) for level in levels]
    total = functools.reduce(jnp.add, parts)
    scale = 1.0 / total
    return [part * scale for part in parts], peak + jnp.log2(total)


def kernel(
    lengths_hbm,
    q_nope_hbm,
    q_rope_hbm,
    ids_hbm,
    gates_hbm,
    cache_hbm,
    absorb_hbm,
    value_hbm,
    output_hbm,
    gate_hbm,
    up_hbm,
    down_hbm,
    out_ref,
    lengths_ref,
    q_nope_ref,
    q_rope_ref,
    ids_ref,
    gates_ref,
    keys2,
    keys4,
    values_a,
    values_b,
    absorb,
    value_up,
    w_out,
    w_gate,
    w_up,
    w_down,
    query2,
    query4,
    s1_2,
    r1_2,
    s1_4,
    r1_4,
    whole,
    whole_level,
    s3,
    r3,
    s4,
    r4,
    heads,
    s5,
    r5,
    s6,
    r6,
    s7,
    r7,
    s8,
    r8,
    key_sem,
    weight_sem,
    query2_sem,
    query4_send,
    query4_recv,
    s1_2_sem,
    r1_2_sem,
    s1_4_sem,
    r1_4_sem,
    s3_sem,
    r3_sem,
    s4_sem,
    r4_sem,
    s5_sem,
    r5_sem,
    s6_sem,
    r6_sem,
    s7_sem,
    r7_sem,
    s8_sem,
    r8_sem,
):
    ctx = lax.axis_index("ctx")
    head = lax.axis_index("head")
    keys = {2: keys2, 4: keys4}
    query = {2: query2, 4: query4}
    shares = {
        2: (s1_2, r1_2, s1_2_sem, r1_2_sem),
        4: (s1_4, r1_4, s1_4_sem, r1_4_sem),
    }
    place = {sharers: lax.rem(head, sharers) for sharers in (2, 4)}

    def partner(sharers, step):
        member = lax.rem(place[sharers] + step, sharers)
        return member, {"head": head - place[sharers] + member}

    def other_ctx(step):
        dy, dx = step
        return lax.rem(ctx // 4 + dy, 4) * 4 + lax.rem(lax.rem(ctx, 4) + dx, 4)

    def other_head(step):
        return lax.rem(head + step, HEAD)

    def slot(row):
        chunk = row // CHUNK
        return keys[SHARERS[chunk]].at[FIRST[chunk] + row % CHUNK]

    def key_copy(row):
        sharers = SHARERS[row // CHUNK]
        span = SLICE // sharers
        positions = pl.ds(pl.multiple_of(place[sharers] * span, span), span)
        return pltpu.make_async_copy(
            cache_hbm.at[row, :, positions], slot(row), key_sem.at[row]
        )

    absorb_copy = pltpu.make_async_copy(absorb_hbm, absorb, weight_sem.at[0])
    value_copy = pltpu.make_async_copy(value_hbm, value_up, weight_sem.at[1])
    output_copy = pltpu.make_async_copy(output_hbm, w_out.at[pl.ds(0, COLS)], weight_sem.at[2])
    gate_copy = pltpu.make_async_copy(gate_hbm.at[0], w_gate, weight_sem.at[3])
    up_copy = pltpu.make_async_copy(up_hbm.at[0], w_up, weight_sem.at[4])
    down_copy = pltpu.make_async_copy(down_hbm.at[0], w_down, weight_sem.at[5])
    small_copies = [
        pltpu.make_async_copy(src, dst, weight_sem.at[6 + index])
        for index, (src, dst) in enumerate(
            (
                (q_nope_hbm, q_nope_ref),
                (q_rope_hbm, q_rope_ref),
                (lengths_hbm, lengths_ref),
                (ids_hbm, ids_ref),
                (gates_hbm, gates_ref),
            )
        )
    ]
    small_copies[0].start()
    absorb_copy.start()
    for copy in small_copies[1:]:
        copy.start()
    for row in range(2):
        key_copy(row).start()
    barrier = pltpu.get_barrier_semaphore()

    def greet(device):
        pl.semaphore_signal(barrier, inc=1, device_id=device, device_id_type=MESH)

    for step in FARTHEST:
        greet({"ctx": other_ctx(step)})
    loop(1, HEAD, lambda step: greet({"head": other_head(step)}))
    for row in range(2, 6):
        key_copy(row).start()
    value_copy.start()
    output_copy.start()
    for row in range(6, ROWS):
        key_copy(row).start()
    gate_copy.start()
    up_copy.start()
    down_copy.start()

    w_out[pl.ds(COLS, 512 - COLS), :] = jnp.zeros((512 - COLS, GROUP * NOPE), BF16)
    small_copies[0].wait()
    flat = q_nope_ref[...].reshape(ROWS * GROUP, NOPE).astype(F32)
    which = lax.rem(lax.broadcasted_iota(jnp.int32, (ROWS * GROUP, NOPE), 0), GROUP)
    blocks = [jnp.where(which == h, flat, 0.0).astype(BF16) for h in range(GROUP)]
    wide_query = jnp.concatenate(blocks, axis=1)
    absorb_copy.wait()
    latent = jnp.dot(
        wide_query,
        absorb[...].reshape(GROUP * NOPE, LAT),
        preferred_element_type=F32,
    ).astype(BF16)
    latent = latent.reshape(ROWS, GROUP, LAT)
    small_copies[1].wait()

    def mine(sharers):
        return pl.ds(pl.multiple_of(place[sharers] * GROUP, GROUP), GROUP)

    for chunk in range(CHUNKS):
        held = query[SHARERS[chunk]]
        here = pl.ds(FIRST[chunk], CHUNK)
        rows = slice(chunk * CHUNK, (chunk + 1) * CHUNK)
        held[here, mine(SHARERS[chunk]), 0:LAT] = latent[rows]
        held[here, mine(SHARERS[chunk]), LAT:KEY] = q_rope_ref[rows]
    pl.semaphore_wait(barrier, HEAD - 1 + CTX - 1)
    block2 = query2.at[:, mine(2)]
    query2_copy = remote(
        block2, block2, query2_sem.at[0], query2_sem.at[1], partner(2, 1)[1]
    )
    query2_copy.start()

    def query4_copy(chunk, step, arrival=False):
        member, device = partner(4, step)
        owner = member if arrival else place[4]
        rows = pl.ds(FIRST[chunk], CHUNK)
        block = query4.at[rows, pl.ds(pl.multiple_of(owner * GROUP, GROUP), GROUP)]
        return remote(
            block,
            block,
            query4_send.at[FIRST[chunk] // CHUNK, member],
            query4_recv.at[FIRST[chunk] // CHUNK, owner],
            device,
        )

    for chunk in (1, 2):
        for step in (1, 2, 3):
            query4_copy(chunk, step).start()
    for copy in small_copies[2:]:
        copy.wait()

    def scores(row):
        chunk = row // CHUNK
        sharers = SHARERS[chunk]
        span = SLICE // sharers
        position = ctx * SLICE + place[sharers] * span + lanes((1, span))
        heads_of_row = query[sharers][FIRST[chunk] + row % CHUNK]
        score = jnp.dot(heads_of_row, slot(row)[...], preferred_element_type=F32)
        return jnp.where(position < lengths_ref[row], score, -1e30)

    def soften(score):
        peak = jnp.max(score, axis=1, keepdims=True)
        weight = jnp.exp2((score - peak) * SCALE)
        total = jnp.sum(weight, axis=1, keepdims=True)
        return weight.astype(BF16), 1.0 / total, peak * SCALE + jnp.log2(total)

    def turn(row, values):
        values[0 : SLICE // SHARERS[row // CHUNK], :] = slot(row)[0:LAT, :].T

    def average(weight, values, inverse):
        held = values[0 : weight.shape[1], :]
        return jnp.dot(weight, held, preferred_element_type=F32) * inverse

    key_copy(0).wait()
    turn(0, values_a)
    query2_copy.wait_recv()

    def nothing():
        pass

    def attend_pair(chunk, beside):
        first = chunk * CHUNK
        more = chunk + 1 < CHUNKS
        key_copy(first + 1).wait()
        beside()
        score = scores(first)
        turn(first + 1, values_b)
        weight, inverse, level_a = soften(score)
        score = scores(first + 1)
        if more:
            key_copy(first + 2).wait()
        summed_a = average(weight, values_a, inverse)
        if more:
            turn(first + 2, values_a)
        weight, inverse, level_b = soften(score)
        summed_b = average(weight, values_b, inverse)
        return (summed_a, level_a), (summed_b, level_b)

    def share_copy(chunk, step, arrival=False):
        sharers = SHARERS[chunk]
        src, dst, send_sem, recv_sem = shares[sharers]
        member, device = partner(sharers, step)
        source = member if arrival else place[sharers]
        index = FIRST[chunk] // CHUNK
        return remote(
            src.at[index, member],
            dst.at[index, source],
            send_sem.at[index, member],
            recv_sem.at[index, source],
            device,
        )

    def attend(chunk, beside=nothing):
        sharers = SHARERS[chunk]
        if sharers == 4:
            for step in (1, 2, 3):
                query4_copy(chunk, step, True).wait_recv()
        results = attend_pair(chunk, beside)
        src = shares[sharers][0]
        index = FIRST[chunk] // CHUNK
        level = put_levels([result[1] for result in results], sharers * GROUP)
        for group in range(sharers):
            rows = slice(group * GROUP, (group + 1) * GROUP)
            for row in range(CHUNK):
                for tile in range(4):
                    src[index, group, row * 4 + tile] = results[row][0][
                        rows, tile * 128 : (tile + 1) * 128
                    ].astype(BF16)
            src[index, group, CHUNK * 4] = level[rows].astype(BF16)
        for step in range(sharers - 1, 0, -1):
            share_copy(chunk, step).start()

    def receive_shares(chunk):
        for step in range(1, SHARERS[chunk]):
            share_copy(chunk, step, True).wait_recv()

    def merge_shares(chunk):
        sharers = SHARERS[chunk]
        src, dst = shares[sharers][0:2]
        index = FIRST[chunk] // CHUNK
        blocks = [src.at[index, place[sharers]]]
        for step in range(1, sharers):
            blocks.append(dst.at[index, partner(sharers, step)[0]])
        tiles = [block[CHUNK * 4].astype(F32) for block in blocks]
        for row in range(CHUNK):
            parts, level = weights_of([get_level(tile, row) for tile in tiles])
            rows = pl.ds((chunk * CHUNK + row) * GROUP, GROUP)
            for tile in range(4):
                whole[rows, tile * 128 : (tile + 1) * 128] = functools.reduce(
                    jnp.add,
                    [
                        block[row * 4 + tile].astype(F32) * part
                        for block, part in zip(blocks, parts)
                    ],
                )
            whole_level[rows, :] = jnp.broadcast_to(level, (GROUP, 128))

    def to_ctx(src, dst, send_sem, recv_sem, step):
        peer = other_ctx(step)
        return remote(src(peer), dst.at[ctx], send_sem.at[peer], recv_sem.at[ctx], {"ctx": peer})

    def from_ctx(src, dst, send_sem, recv_sem, step):
        peer = other_ctx(step)
        return remote(src(peer), dst.at[peer], send_sem.at[peer], recv_sem.at[peer], {"ctx": peer})

    def to_head(src, dst, send_sem, recv_sem, step):
        peer = other_head(step)
        return remote(src(peer), dst.at[head], send_sem.at[peer], recv_sem.at[head], {"head": peer})

    def from_head(src, dst, send_sem, recv_sem, step):
        peer = other_head(step)
        return remote(src(peer), dst.at[peer], send_sem.at[peer], recv_sem.at[peer], {"head": peer})

    exchange3 = (lambda peer: s3, r3, s3_sem, r3_sem)
    exchange4 = (lambda peer: s4, r4, s4_sem, r4_sem)
    exchange5 = (lambda peer: s5, r5, s5_sem, r5_sem)
    exchange6 = (lambda peer: s6, r6, s6_sem, r6_sem)
    exchange7 = (lambda peer: s7.at[peer], r7, s7_sem, r7_sem)
    exchange8 = (lambda peer: s8.at[peer], r8, s8_sem, r8_sem)

    def send_ctx(exchange):
        for step in FARTHEST:
            to_ctx(*exchange, step).start()

    def receive_ctx(exchange):
        for step in NEAREST:
            from_ctx(*exchange, step).wait_recv()

    def project(first, count, exchange):
        rows = pl.ds(first * GROUP, count * GROUP)
        merged = whole[rows, :]
        which = lax.rem(lax.broadcasted_iota(jnp.int32, (count * GROUP, LAT), 0), GROUP)
        blocks = [jnp.where(which == h, merged, 0.0).astype(BF16) for h in range(GROUP)]
        share = jnp.dot(
            jnp.concatenate(blocks, axis=1),
            value_up[...].reshape(GROUP * LAT, NOPE),
            preferred_element_type=F32,
        ).astype(BF16)
        src = exchange[0](0)
        src[0:count] = share.reshape(count, GROUP, NOPE)
        levels = [whole_level[pl.ds((first + row) * GROUP, GROUP), :] for row in range(count)]
        src[count] = put_levels(levels, GROUP).astype(BF16)
        send_ctx(exchange)
        exchange[1][ctx] = src[...]

    def merge_ctx(first, count, exchange):
        receive_ctx(exchange)
        arrived = exchange[1]
        tiles = [arrived[peer, count].astype(F32) for peer in range(CTX)]
        for row in range(count):
            parts, _ = weights_of([get_level(tile, row) for tile in tiles])
            heads[pl.ds((first + row) * GROUP, GROUP), :] = functools.reduce(
                jnp.add, [arrived[peer, row].astype(F32) * parts[peer] for peer in range(CTX)]
            )

    attend(0)
    attend(1)
    receive_shares(0)
    attend(2, lambda: merge_shares(0))
    value_copy.wait()
    receive_shares(1)
    merge_shares(1)
    project(0, EARLY, exchange3)
    attend(3)
    receive_shares(2)
    merge_shares(2)
    receive_shares(3)
    merge_shares(3)
    project(EARLY, LATE, exchange4)
    output_copy.wait()
    values_a[0 : GROUP * NOPE, :] = w_out[...].T
    merge_ctx(0, EARLY, exchange3)
    merge_ctx(EARLY, LATE, exchange4)
    gathered = [heads[pl.ds(member, ROWS, stride=GROUP), :] for member in range(GROUP)]
    partial = jnp.dot(
        jnp.concatenate(gathered, axis=1).astype(BF16),
        values_a[0 : GROUP * NOPE, :],
        preferred_element_type=F32,
    )
    s5[0], s5[1] = pack(partial)
    for step in HEAD_STEPS:
        to_head(*exchange5, step).start()
    r5[head] = s5[...]
    query2_copy.wait_send()
    for chunk in range(CHUNKS):
        for step in range(1, SHARERS[chunk]):
            if SHARERS[chunk] == 4:
                query4_copy(chunk, step).wait_send()
            share_copy(chunk, step).wait_send()
    for exchange in (exchange3, exchange4):
        for step in NEAREST:
            to_ctx(*exchange, step).wait_send()
    for step in HEAD_STEPS[::-1]:
        from_head(*exchange5, step).wait_recv()
    attn = functools.reduce(jnp.add, [unpack(r5[peer, 0], r5[peer, 1]) for peer in range(HEAD)])
    s6[0], s6[1] = pack(attn)
    send_ctx(exchange6)
    r6[ctx] = s6[...]
    out_ref[:, 0:512] = attn
    gate_copy.wait()
    up_copy.wait()
    squares = jnp.zeros((ROWS, 512), F32)
    gate = jnp.zeros((ROWS, 256), F32)
    upper = jnp.zeros((ROWS, 256), F32)
    for step in [(0, 0)] + NEAREST:
        peer = other_ctx(step)
        if step != (0, 0):
            from_ctx(*exchange6, step).wait_recv()
        features = unpack(r6[peer, 0], r6[peer, 1])
        squares += features * features
        features = features[:, 0:COLS].astype(BF16)
        rows = pl.ds(pl.multiple_of(peer * COLS, COLS), COLS)
        gate += jnp.dot(features, w_gate[rows, :], preferred_element_type=F32)
        upper += jnp.dot(features, w_up[rows, :], preferred_element_type=F32)
    mean = jnp.sum(squares, axis=1, keepdims=True) * (1.0 / D)
    factor = 1.0 / jnp.sqrt(mean + 1e-06)
    gate = gate * factor
    upper = upper * factor
    hidden = (gate / (1.0 + jnp.exp(-gate)) * upper).astype(BF16)
    chosen = jnp.where(ids_ref[...] == ctx, gates_ref[...], 0.0)
    select = jnp.sum(chosen, axis=1, keepdims=True)
    down_copy.wait()
    result = jnp.dot(hidden, w_down[...], preferred_element_type=F32) * select
    for peer in range(CTX):
        left = peer * COLS // 128 * 128
        s7[peer, 0], s7[peer, 1] = pack(result[:, left : left + 512])
    send_ctx(exchange7)
    share = unpack(s7[ctx, 0], s7[ctx, 1])
    for step in NEAREST:
        peer = other_ctx(step)
        from_ctx(*exchange7, step).wait_recv()
        share += unpack(r7[peer, 0], r7[peer, 1])
    share = jnp.where(lax.rem(ctx, 2) == 1, pltpu.roll(share, 512 - COLS % 128, 1), share)
    for peer in range(HEAD):
        moved = share if peer == 0 else pltpu.roll(share, 512 - peer * OUT, 1)
        s8[peer] = moved[:, 0:128]
    for step in HEAD_STEPS:
        to_head(*exchange8, step).start()
    r8[head] = s8[head]
    for exchange in (exchange6, exchange7):
        for step in NEAREST:
            to_ctx(*exchange, step).wait_send()
    for step in HEAD_STEPS:
        to_head(*exchange5, step).wait_send()
        to_head(*exchange8, step).wait_send()
    for step in HEAD_STEPS[::-1]:
        from_head(*exchange8, step).wait_recv()
    out_ref[:, 512:640] = functools.reduce(jnp.add, [r8[peer] for peer in range(HEAD)])


def finish(both_ref, attn_ref, expert_ref):
    attn_ref[...] = both_ref[:, 0:COLS].astype(BF16)
    expert_ref[...] = both_ref[:, 512 : 512 + OUT].astype(BF16)


def body(
    q_nope,
    q_rope,
    latent_cache,
    lengths,
    w_key_absorb,
    w_value_up,
    w_output,
    w_gate,
    w_up,
    w_down,
    expert_ids,
    gate_weights,
):
    vmem = pl.BlockSpec(memory_space=pltpu.VMEM)
    hbm = pl.BlockSpec(memory_space=pl.ANY)
    dma = pltpu.SemaphoreType.DMA
    both = pl.pallas_call(
        kernel,
        out_shape=pltpu.VMEM((ROWS, 640), F32),
        in_specs=[hbm] * 12,
        out_specs=vmem,
        scratch_shapes=[
            pltpu.SMEM((ROWS,), jnp.int32),
            pltpu.VMEM((ROWS, GROUP, NOPE), BF16),
            pltpu.VMEM((ROWS, GROUP, ROPE), BF16),
            pltpu.VMEM((ROWS, 8), jnp.int32),
            pltpu.VMEM((ROWS, 8), F32),
            pltpu.VMEM((4, KEY, SLICE // 2), BF16),
            pltpu.VMEM((4, KEY, SLICE // 4), BF16),
            pltpu.VMEM((SLICE // 2, LAT), BF16),
            pltpu.VMEM((SLICE // 2, LAT), BF16),
            pltpu.VMEM((GROUP, NOPE, LAT), BF16),
            pltpu.VMEM((GROUP, LAT, NOPE), BF16),
            pltpu.VMEM((512, GROUP * NOPE), BF16),
            pltpu.VMEM((D, 256), BF16),
            pltpu.VMEM((D, 256), BF16),
            pltpu.VMEM((256, D), BF16),
            pltpu.VMEM((4, 2 * GROUP, KEY), BF16),
            pltpu.VMEM((4, 4 * GROUP, KEY), BF16),
            pltpu.VMEM((2, 2, TILES, 16, 128), BF16),
            pltpu.VMEM((2, 2, TILES, 16, 128), BF16),
            pltpu.VMEM((2, 4, TILES, 16, 128), BF16),
            pltpu.VMEM((2, 4, TILES, 16, 128), BF16),
            pltpu.VMEM((ROWS * GROUP, LAT), F32),
            pltpu.VMEM((ROWS * GROUP, 128), F32),
            pltpu.VMEM((EARLY + 1, 16, 128), BF16),
            pltpu.VMEM((CTX, EARLY + 1, 16, 128), BF16),
            pltpu.VMEM((LATE + 1, 16, 128), BF16),
            pltpu.VMEM((CTX, LATE + 1, 16, 128), BF16),
            pltpu.VMEM((ROWS * GROUP, NOPE), F32),
            pltpu.VMEM((2, 16, 128), BF16),
            pltpu.VMEM((HEAD, 2, 16, 128), BF16),
            pltpu.VMEM((2, 16, 128), BF16),
            pltpu.VMEM((CTX, 2, 16, 128), BF16),
            pltpu.VMEM((CTX, 2, 16, 128), BF16),
            pltpu.VMEM((CTX, 2, 16, 128), BF16),
            pltpu.VMEM((HEAD, ROWS, 128), F32),
            pltpu.VMEM((HEAD, ROWS, 128), F32),
            dma((ROWS,)),
            dma((11,)),
            dma((2,)),
            dma((2, 4)),
            dma((2, 4)),
            dma((2, 2)),
            dma((2, 2)),
            dma((2, 4)),
            dma((2, 4)),
            dma((CTX,)),
            dma((CTX,)),
            dma((CTX,)),
            dma((CTX,)),
            dma((HEAD,)),
            dma((HEAD,)),
            dma((CTX,)),
            dma((CTX,)),
            dma((CTX,)),
            dma((CTX,)),
            dma((HEAD,)),
            dma((HEAD,)),
        ],
        compiler_params=pltpu.CompilerParams(
            collective_id=0, has_side_effects=True, vmem_limit_bytes=60 * 2**20
        ),
    )(
        lengths,
        q_nope,
        q_rope,
        expert_ids,
        gate_weights,
        jnp.swapaxes(latent_cache, 1, 2),
        w_key_absorb,
        w_value_up,
        w_output.T,
        w_gate,
        w_up,
        w_down,
    )
    return pl.pallas_call(
        finish,
        out_shape=(
            jax.ShapeDtypeStruct((ROWS, COLS), BF16),
            jax.ShapeDtypeStruct((ROWS, OUT), BF16),
        ),
        compiler_params=pltpu.CompilerParams(vmem_limit_bytes=2**20),
    )(both)


def solution(mesh):
    return jax.shard_map(
        body,
        mesh=mesh,
        in_specs=(
            P(None, "head", None),
            P(None, "head", None),
            P(None, "ctx", None),
            P(),
            P("head", None, None),
            P("head", None, None),
            P("head", "ctx"),
            P("ctx", None, "head"),
            P("ctx", None, "head"),
            P("ctx", "head", None),
            P(),
            P(),
        ),
        out_specs=(P(None, "ctx"), P(None, ("ctx", "head"))),
        check_vma=False,
    )
```
